32 devices in a mesh: dp: 4 (over y, x), shard: 8 (over z, core).
Axes of the slice: x: 2, y: 2, z: 4, core: 2. Of those that a mesh axis runs over, the one named last changes fastest.
Arguments:
- training_inputs: bfloat16 [4096, 8192], P(('dp', 'shard')), may hold values from -6 to 6
- training_cotangents: bfloat16 [4096, 8192], P(('dp', 'shard')), may hold values from -6 to 6
- validation_inputs: bfloat16 [1024, 8192], P(('dp', 'shard')), may hold values from -6 to 6
- validation_cotangents: bfloat16 [1024, 8192], P(('dp', 'shard')), may hold values from -6 to 6
- adapter_down: bfloat16 [8192, 64], replicated, may hold values from -0.0625 to 0.0625
- adapter_up: bfloat16 [64, 8192], replicated, may hold values from -0.0625 to 0.0625
- adam_first_moment: bfloat16 [8, 128, 1024], P('shard'), may hold values from -6 to 6
- adam_second_moment: bfloat16 [8, 128, 1024], P('shard'), may hold values from 0.019897461 to 20
- slot_block_index: int32 [8], replicated, may hold values from 0 to 7, each once
- example_lengths: int32 [4, 8, 8], P('dp', 'shard'), may hold values from 1 to 64, 128 in all within a row
- projection_rows: float32 [128, 64], replicated, may hold values from -0.5 to 0.5
- projection_columns: float32 [8192, 128], replicated, may hold values from -0.0625 to 0.0625
Outputs:
- train_dirs: float32 [4, 8, 8, 8192], P('dp', 'shard')
- val_dir: float32 [8192], replicated
- scores: float32 [4, 8, 8], P('dp', 'shard')
The draws below stay inside these ranges and needn't reach their ends.
Inputs may be any that keep to these rules, and one draw needn't show every extreme that they name: slot_block_index holds every block number once. `example_lengths`: each device's 8 lengths sum to 128; on every device the longest example has exactly 64 tokens.
All inputs are finite; a program needn't handle non-finite values.
Results may differ from the reference program's by a relative error of at most 0.015.
Values may be sent and summed in bfloat16 or wider, within the bound.
No kernel may reach another device: no remote copies, remote signals or barrier semaphores. Data moves between devices by JAX's collectives and lax.ppermute only.
A program may use at most 192 MiB of HBM per device.

```python
import math
import jax
import jax.numpy as jnp
import numpy as np
from jax import lax

MODEL_WIDTH = 8192
ADAPTER_RANK = 64
K1 = 64
K2 = 128
TOKENS_DEVICE = 128
EXAMPLES_DEVICE = 8
BLOCKS = 8
W = 1024
GROUPS = 4
SCORERS = 8
TOKENS = 4096
VAL_TOKENS = 1024


def block_scale(own_key, dims, cuts, smallest, top_value):
    def one(dim, shards_of):
        draws = jax.random.uniform(jax.random.fold_in(jax.random.fold_in(own_key, 6), dim), (shards_of,), jnp.float32, smallest / len(cuts), top_value / len(cuts))
        return jnp.repeat(jnp.exp(draws), dims[dim] // shards_of).reshape((-1,) + (1,) * (len(dims) - dim - 1))

    level = one(*cuts[0])
    for cut in cuts[1:]:
        level = level * one(*cut)
    return level


def profile(count, total, reach, lean):
    loads = [(1 << 20) // math.isqrt(rank ** lean) + 1 for rank in range(2, count + 1)]
    spare, holding = total - reach - (count - 1), [1] * (count - 1)
    while spare > 0:
        candidates = [i for i in range(count - 1) if holding[i] < reach]
        whole, left = sum([loads[i] for i in candidates]), spare
        for i in candidates:
            extra = min(reach - holding[i], max(1, left * loads[i] // whole), spare)
            holding[i] = holding[i] + extra
            spare = spare - extra
    return np.array([reach] + holding)


def uneven(own_key, number_of, total, reach, slope):
    if number_of == 2:
        one = jax.random.randint(own_key, (), max(1, total - reach), min(reach, total - 1) + 1)
        return jnp.stack([one, total - one])
    sizes = jnp.asarray(profile(number_of, total, reach, slope), jnp.int32)
    pairs = (number_of - 1) // 2
    source_of, sink = sizes[1:1 + 2 * pairs:2], sizes[2:2 + 2 * pairs:2]
    slack = jnp.minimum(source_of - 1, reach - sink)
    moved = jax.random.randint(jax.random.fold_in(own_key, 1), (pairs,), 0, 1 << 20) % (slack + 1)
    sizes = sizes.at[1:1 + 2 * pairs:2].set(source_of - moved).at[2:2 + 2 * pairs:2].set(sink + moved)
    return sizes[jax.random.permutation(jax.random.fold_in(own_key, 2), number_of)]


def gaussian(stream_key, extent, spread, limit, split=(), held_as=jnp.bfloat16):
    loudness = block_scale(stream_key, extent, split, -0.22, 0.18) if split else 1.0
    drawn = jax.random.normal(stream_key, extent, jnp.float32) * spread * loudness
    return jnp.minimum(jnp.maximum(drawn, -limit), limit).astype(held_as)


def setup_inputs(seed: int = 0) -> dict:
    arg_keys = jax.random.split(jax.random.key(seed), 13)
    return {
        "training_inputs": gaussian(arg_keys[0], (TOKENS, MODEL_WIDTH), 1.0, 6.0, ((0, 32),)),
        "training_cotangents": gaussian(arg_keys[1], (TOKENS, MODEL_WIDTH), 1.0, 6.0, ((0, 32),)),
        "validation_inputs": gaussian(arg_keys[2], (VAL_TOKENS, MODEL_WIDTH), 1.0, 6.0, ((0, 32),)),
        "validation_cotangents": gaussian(arg_keys[3], (VAL_TOKENS, MODEL_WIDTH), 1.0, 6.0, ((0, 32),)),
        "adapter_down": gaussian(arg_keys[4], (MODEL_WIDTH, ADAPTER_RANK), MODEL_WIDTH ** -0.5, 0.0625),
        "adapter_up": gaussian(arg_keys[5], (ADAPTER_RANK, MODEL_WIDTH), MODEL_WIDTH ** -0.5, 0.0625),
        "adam_first_moment": gaussian(arg_keys[6], (BLOCKS, 2 * ADAPTER_RANK, W), 1.0, 6.0, ((0, 8),)),
        "adam_second_moment": jnp.clip(jnp.exp(math.log(20.0) - 6.912895 * jax.random.uniform(arg_keys[7], (BLOCKS, 2 * ADAPTER_RANK, W), jnp.float32) ** block_scale(arg_keys[7], (BLOCKS, 2 * ADAPTER_RANK, W), ((0, 8),), -0.2, 0.2)), 0.019897461, 20.0).astype(jnp.bfloat16),
        "slot_block_index": jax.random.permutation(arg_keys[8], BLOCKS).astype(jnp.int32),
        "example_lengths": jax.vmap(lambda own: uneven(own, EXAMPLES_DEVICE, TOKENS_DEVICE, TOKENS_DEVICE // 2, 2))(jax.random.split(arg_keys[9], GROUPS * SCORERS)).reshape((GROUPS, SCORERS, EXAMPLES_DEVICE)).astype(jnp.int32),
        "projection_rows": gaussian(arg_keys[10], (2 * ADAPTER_RANK, K1), (2 * ADAPTER_RANK) ** -0.5, 0.5, (), jnp.float32),
        "projection_columns": gaussian(arg_keys[11], (MODEL_WIDTH, K2), MODEL_WIDTH ** -0.5, 0.0625, (), jnp.float32),
    }


beta_first = 0.9
beta_second = 0.999
epsilon = 1e-06

def membership(lengths, total_rows):
    finish = jnp.cumsum(lengths)
    begins = finish - lengths
    position = jnp.arange(total_rows, dtype=jnp.int32)[:, None]
    return ((position >= begins[None, :]) & (position < finish[None, :])).astype(jnp.bfloat16)

def reduced_rank(input_rows, output_cotangent, adapter_down, adapter_up):
    backward_adapter = jnp.dot(output_cotangent, adapter_up.T, preferred_element_type=jnp.float32).astype(jnp.bfloat16)
    forward_adapter = jnp.dot(input_rows, adapter_down, preferred_element_type=jnp.float32).astype(jnp.bfloat16)
    return (backward_adapter, forward_adapter)

def normalize(vector):
    return vector / jnp.sqrt(lax.optimization_barrier(jnp.mean(vector * vector, axis=-1, keepdims=True)) + epsilon)

def project(gradient, projection_rows, columns):
    inner = jnp.dot(gradient, columns, precision=lax.Precision.HIGHEST)
    return jnp.einsum('rj,rk->jk', projection_rows, inner, precision=lax.Precision.HIGHEST)

def reference(training_inputs, training_cotangents, validation_inputs, validation_cotangents, adapter_down, adapter_up, adam_first_moment, adam_second_moment, slot_block_index, example_lengths, projection_rows, projection_columns):
    adapter_rank = adapter_down.shape[1]
    sorted_first_moment = jnp.zeros_like(adam_first_moment).at[slot_block_index].set(adam_first_moment)
    sorted_second_moment = jnp.zeros_like(adam_second_moment).at[slot_block_index].set(adam_second_moment)
    moment_first_slot = sorted_first_moment.astype(jnp.float32).transpose(1, 0, 2).reshape(2 * adapter_rank, MODEL_WIDTH)
    moment_second_slot = sorted_second_moment.astype(jnp.float32).transpose(1, 0, 2).reshape(2 * adapter_rank, MODEL_WIDTH)
    validation_backward, validation_forward = reduced_rank(validation_inputs, validation_cotangents, adapter_down, adapter_up)
    val_grad = jnp.concatenate([jnp.dot(validation_backward.T, validation_inputs, preferred_element_type=jnp.float32), jnp.dot(validation_forward.T, validation_cotangents, preferred_element_type=jnp.float32)], axis=0)
    val_dir = normalize(project(val_grad, projection_rows, projection_columns).reshape(K1 * K2))
    inputs_all = training_inputs.reshape(GROUPS * SCORERS, TOKENS_DEVICE, MODEL_WIDTH)
    cotangent_all = training_cotangents.reshape(GROUPS * SCORERS, TOKENS_DEVICE, MODEL_WIDTH)
    lengths_all = example_lengths.reshape(GROUPS * SCORERS, EXAMPLES_DEVICE)

    def one_device(packed):
        input_rows, output_cotangent, lengths = packed
        backward_adapter, forward_adapter = reduced_rank(input_rows, output_cotangent, adapter_down, adapter_up)
        member_flag = membership(lengths, TOKENS_DEVICE)
        masked_backward = (backward_adapter[:, None, :] * member_flag[:, :, None]).reshape(TOKENS_DEVICE, EXAMPLES_DEVICE * adapter_rank)
        forward_masked = (forward_adapter[:, None, :] * member_flag[:, :, None]).reshape(TOKENS_DEVICE, EXAMPLES_DEVICE * adapter_rank)
        top_half = jnp.dot(masked_backward.T, input_rows, preferred_element_type=jnp.float32).reshape(EXAMPLES_DEVICE, adapter_rank, MODEL_WIDTH)
        bottom_half = jnp.dot(forward_masked.T, output_cotangent, preferred_element_type=jnp.float32).reshape(EXAMPLES_DEVICE, adapter_rank, MODEL_WIDTH)
        gradient = jnp.concatenate([top_half, bottom_half], axis=1)
        update = (beta_first * moment_first_slot[None] + (1 - beta_first) * gradient) / jnp.sqrt(beta_second * moment_second_slot[None] + (1 - beta_second) * gradient * gradient)
        inner = jnp.einsum('erd,dk->erk', update, projection_columns, precision=lax.Precision.HIGHEST)
        projected = jnp.einsum('rj,erk->ejk', projection_rows, inner, precision=lax.Precision.HIGHEST)
        return normalize(projected.reshape(EXAMPLES_DEVICE, K1 * K2))
    directions = lax.map(one_device, (inputs_all, cotangent_all, lengths_all))
    directions = directions.reshape(GROUPS, SCORERS, EXAMPLES_DEVICE, K1 * K2)
    scores = lax.optimization_barrier(jnp.sum(directions * val_dir, axis=-1)) / math.sqrt(K1 * K2)
    return (directions, val_dir, scores)
```

```python
import functools
import math

import jax
import jax.numpy as jnp
from jax import lax
from jax.experimental import pallas as pl
from jax.experimental.pallas import tpu as pltpu
from jax.sharding import PartitionSpec as P

epsilon = 1e-06
update_scale = 0.1 / math.sqrt(0.001)
HIGHEST = lax.Precision.HIGHEST
TN = (((0,), (0,)), ((), ()))
NT = (((1,), (1,)), ((), ()))


def mm(a, b, dims=(((1,), (0,)), ((), ())), precision=None):
    return lax.dot_general(a, b, dims, precision=precision, preferred_element_type=jnp.float32)


def prepare_kernel(
    lengths, x, g, xv, gv, down, up, columns, rows,
    columns_out, top_out, bottom_out, proj_out,
    back, fwd, vback, vfwd, xc, gc,
):
    step = pl.program_id(0)

    @pl.when(step == 0)
    def _():
        for total in (back, fwd, vback, vfwd, xc, gc):
            total[...] = jnp.zeros_like(total)

    k2 = columns.shape[1]
    exact = columns[...]
    coarse = exact.astype(jnp.bfloat16)
    fine = (exact - coarse.astype(jnp.float32)).astype(jnp.bfloat16)
    table = jnp.concatenate([coarse, fine], axis=1)
    columns_out[...] = table
    back[...] += mm(g[...], up[...], NT)
    fwd[...] += mm(x[...], down[...])
    vback[...] += mm(gv[...], up[...], NT)
    vfwd[...] += mm(xv[...], down[...])
    xc[...] += mm(xv[...], table)
    gc[...] += mm(gv[...], table)

    @pl.when(step == pl.num_programs(0) - 1)
    def _():
        rank = back.shape[1]
        tokens = back.shape[0]
        position = lax.broadcasted_iota(jnp.int32, (rank, tokens), 1)
        back_t = back[...].T
        fwd_t = fwd[...].T
        begin = jnp.int32(0)
        for e in range(lengths.shape[0]):
            finish = begin + lengths[e]
            member = (position >= begin) & (position < finish)
            top_out[pl.ds(e * rank, rank), :] = jnp.where(member, back_t, 0.0).astype(jnp.bfloat16)
            bottom_out[pl.ds(e * rank, rank), :] = jnp.where(member, fwd_t, 0.0).astype(jnp.bfloat16)
            begin = finish
        round_b = vback[...].astype(jnp.bfloat16).astype(jnp.float32)
        round_f = vfwd[...].astype(jnp.bfloat16).astype(jnp.float32)
        inner_top = mm(round_b, xc[:, :k2] + xc[:, k2:], TN, HIGHEST)
        inner_bottom = mm(round_f, gc[:, :k2] + gc[:, k2:], TN, HIGHEST)
        proj_out[...] = mm(rows[pl.ds(0, rank), :], inner_top, TN, HIGHEST) + mm(
            rows[pl.ds(rank, rank), :], inner_bottom, TN, HIGHEST
        )


def prepare(lengths, x, g, xv, gv, down, up, columns, rows):
    tokens, width = x.shape
    val_tokens = xv.shape[0]
    rank = down.shape[1]
    k1, k2 = rows.shape[1], columns.shape[1]
    examples = lengths.shape[0]
    span = 1024
    whole = lambda i: (0, 0)
    across = lambda i: (0, i)
    along = lambda i: (i, 0)
    return pl.pallas_call(
        prepare_kernel,
        grid=(width // span,),
        in_specs=[
            pl.BlockSpec(memory_space=pltpu.SMEM),
            pl.BlockSpec((tokens, span), across),
            pl.BlockSpec((tokens, span), across),
            pl.BlockSpec((val_tokens, span), across),
            pl.BlockSpec((val_tokens, span), across),
            pl.BlockSpec((span, rank), along),
            pl.BlockSpec((rank, span), across),
            pl.BlockSpec((span, k2), along),
            pl.BlockSpec(rows.shape, whole),
        ],
        out_specs=[
            pl.BlockSpec((span, 2 * k2), along),
            pl.BlockSpec((examples * rank, tokens), whole),
            pl.BlockSpec((examples * rank, tokens), whole),
            pl.BlockSpec((k1, k2), whole),
        ],
        out_shape=[
            jax.ShapeDtypeStruct((width, 2 * k2), jnp.bfloat16),
            jax.ShapeDtypeStruct((examples * rank, tokens), jnp.bfloat16),
            jax.ShapeDtypeStruct((examples * rank, tokens), jnp.bfloat16),
            jax.ShapeDtypeStruct((k1, k2), jnp.float32),
        ],
        scratch_shapes=[
            pltpu.VMEM((tokens, rank), jnp.float32),
            pltpu.VMEM((tokens, rank), jnp.float32),
            pltpu.VMEM((val_tokens, rank), jnp.float32),
            pltpu.VMEM((val_tokens, rank), jnp.float32),
            pltpu.VMEM((val_tokens, 2 * k2), jnp.float32),
            pltpu.VMEM((val_tokens, 2 * k2), jnp.float32),
        ],
        compiler_params=pltpu.CompilerParams(vmem_limit_bytes=32 * 1024 * 1024),
        cost_estimate=pl.CostEstimate(
            flops=4 * tokens * width * rank, bytes_accessed=14_000_000, transcendentals=0
        ),
        name="prepare",
    )(lengths, x, g, xv, gv, down, up, columns, rows)


def update_kernel(
    slots, x, g, table, moments, top, bottom, rows, val_sum,
    dirs_out, val_out, scores_out,
    update, inner,
):
    step = pl.program_id(0)
    rank = rows.shape[0] // 2
    span = x.shape[1]
    examples = top.shape[0] // rank
    quarter = moments.shape[3]
    members = moments.shape[0]

    @pl.when(step == 0)
    def _():
        inner[...] = jnp.zeros_like(inner)

    cut = min(span, 256)
    for half, (source, masked) in enumerate(((x, top), (g, bottom))):
        for c in range(0, span, cut):
            cols = pl.ds(c, cut)
            grad = mm(masked[...], source[:, cols])
            parts = [
                moments[q, 0, :, :, cols].astype(jnp.float32)
                for q in range(half * members // 2, (half + 1) * members // 2)
            ]
            joined = jnp.concatenate(parts, axis=1)
            first = 9.0 * joined[0]
            second = 999.0 * joined[1]
            shared = first * lax.rsqrt(second)
            coarse = shared.astype(jnp.bfloat16)
            update[pl.ds(examples * rank, rank), cols] = coarse
            update[pl.ds((examples + 1) * rank, rank), cols] = (
                shared - coarse.astype(jnp.float32)
            ).astype(jnp.bfloat16)
            for e in range(examples):
                piece = grad[e * rank : (e + 1) * rank]
                change = (first + piece) * lax.rsqrt(second + piece * piece) - shared
                update[pl.ds(e * rank, rank), cols] = change.astype(jnp.bfloat16)
        inner[half] += mm(update[...], table[...])

    @pl.when(step == pl.num_programs(0) - 1)
    def _():
        k2 = inner.shape[2] // 2
        size = rows.shape[1] * k2
        val = val_sum[...]
        val_dir = val * lax.rsqrt(jnp.sum(val * val) / size + epsilon)
        val_out[...] = val_dir
        upper = rows[pl.ds(0, rank), :] * update_scale
        lower = rows[pl.ds(rank, rank), :] * update_scale

        def projected(e):
            part = pl.ds(e * rank, rank)
            folded = [inner[half, part, :k2] + inner[half, part, k2:] for half in (0, 1)]
            return mm(upper, folded[0], TN, HIGHEST) + mm(lower, folded[1], TN, HIGHEST)

        base = projected(examples) + projected(examples + 1)
        for e in range(examples):
            proj = projected(e) + base
            direction = proj * lax.rsqrt(jnp.sum(proj * proj) / size + epsilon)
            dirs_out[e] = direction
            scores_out[e] = jnp.sum(direction * val_dir) / math.sqrt(size)


def update_project(slots, x, g, table, moments, top, bottom, rows, val_sum):
    tokens, width = x.shape
    members, blocks, _, quarter, span = moments.shape
    k1, k2 = rows.shape[1], table.shape[1] // 2
    rank = rows.shape[0] // 2
    examples = top.shape[0] // rank
    whole2 = lambda i, s: (0, 0)
    return pl.pallas_call(
        update_kernel,
        grid_spec=pltpu.PrefetchScalarGridSpec(
            num_scalar_prefetch=1,
            grid=(blocks,),
            in_specs=[
                pl.BlockSpec((tokens, span), lambda i, s: (0, s[i])),
                pl.BlockSpec((tokens, span), lambda i, s: (0, s[i])),
                pl.BlockSpec((span, 2 * k2), lambda i, s: (s[i], 0)),
                pl.BlockSpec((members, 1, 2, quarter, span), lambda i, s: (0, i, 0, 0, 0)),
                pl.BlockSpec(top.shape, whole2),
                pl.BlockSpec(bottom.shape, whole2),
                pl.BlockSpec(rows.shape, whole2),
                pl.BlockSpec(val_sum.shape, whole2),
            ],
            out_specs=[
                pl.BlockSpec((examples, k1, k2), lambda i, s: (0, 0, 0)),
                pl.BlockSpec((k1, k2), whole2),
                pl.BlockSpec(memory_space=pltpu.SMEM),
            ],
            scratch_shapes=[
                pltpu.VMEM(((examples + 2) * rank, span), jnp.bfloat16),
                pltpu.VMEM((2, (examples + 2) * rank, 2 * k2), jnp.float32),
            ],
        ),
        out_shape=[
            jax.ShapeDtypeStruct((examples, k1, k2), jnp.float32),
            jax.ShapeDtypeStruct((k1, k2), jnp.float32),
            jax.ShapeDtypeStruct((examples,), jnp.float32),
        ],
        compiler_params=pltpu.CompilerParams(vmem_limit_bytes=40 * 1024 * 1024),
        cost_estimate=pl.CostEstimate(
            flops=4 * tokens * width * rank * examples, bytes_accessed=12_000_000, transcendentals=0
        ),
        name="update_project",
    )(slots, x, g, table, moments, top, bottom, rows, val_sum)


def body(
    training_inputs,
    training_cotangents,
    validation_inputs,
    validation_cotangents,
    adapter_down,
    adapter_up,
    adam_first_moment,
    adam_second_moment,
    slot_block_index,
    example_lengths,
    projection_rows,
    projection_columns,
):
    members = lax.axis_size("dp")
    quarter = adam_first_moment.shape[1] // members
    start = lax.axis_index("dp") * quarter
    own = jnp.concatenate(
        [
            lax.dynamic_slice_in_dim(adam_first_moment, start, quarter, axis=1),
            lax.dynamic_slice_in_dim(adam_second_moment, start, quarter, axis=1),
        ],
        axis=0,
    )
    gathered = lax.all_gather(own, ("dp", "shard"), axis=0, tiled=False)
    moments = gathered.reshape((members, lax.axis_size("shard")) + own.shape)
    table, top, bottom, val_part = prepare(
        example_lengths[0, 0],
        training_inputs,
        training_cotangents,
        validation_inputs,
        validation_cotangents,
        adapter_down,
        adapter_up,
        projection_columns,
        projection_rows,
    )
    val_sum = lax.psum(val_part, ("dp", "shard"))
    dirs, val_dir, scores = update_project(
        slot_block_index,
        training_inputs,
        training_cotangents,
        table,
        moments,
        top,
        bottom,
        projection_rows,
        val_sum,
    )
    return (
        dirs.reshape(1, 1, dirs.shape[0], -1),
        val_dir.reshape(-1),
        scores[None, None],
    )


def solution(mesh):
    return jax.shard_map(
        body,
        mesh=mesh,
        in_specs=(
            P(("dp", "shard"), None),
            P(("dp", "shard"), None),
            P(("dp", "shard"), None),
            P(("dp", "shard"), None),
            P(),
            P(),
            P("shard", None, None),
            P("shard", None, None),
            P(),
            P("dp", "shard", None),
            P(),
            P(),
        ),
        out_specs=(P("dp", "shard", None, None), P(), P("dp", "shard", None)),
        check_vma=False,
    )
```

```python
import functools
import math

import jax
import jax.numpy as jnp
from jax import lax
from jax.experimental import pallas as pl
from jax.experimental.pallas import tpu as pltpu
from jax.sharding import PartitionSpec as P

epsilon = 1e-06
update_scale = 0.1 / math.sqrt(0.001)
HIGHEST = lax.Precision.HIGHEST
NN = (((1,), (0,)), ((), ()))
TN = (((0,), (0,)), ((), ()))
NT = (((1,), (1,)), ((), ()))
VMEM_LIMIT = 56 * 1024 * 1024
ANY = pl.BlockSpec(memory_space=pl.ANY)
SMEM = pl.BlockSpec(memory_space=pltpu.SMEM)


def mm(a, b, dims=NN, precision=None):
    return lax.dot_general(a, b, dims, precision=precision, preferred_element_type=jnp.float32)


def two_terms(exact):
    coarse = exact.astype(jnp.bfloat16)
    fine = (exact - coarse.astype(jnp.float32)).astype(jnp.bfloat16)
    return coarse, fine


def cut_kernel(place, first, second, out, sems):
    width = out.shape[2]
    cols = pl.ds(pl.multiple_of(place[0] * width, width), width)
    copies = [
        pltpu.make_async_copy(source.at[0, :, cols], out.at[i], sems.at[i])
        for i, source in enumerate((first, second))
    ]
    for copy in copies:
        copy.start()
    for copy in copies:
        copy.wait()


def cut_piece(place, first, second, width):
    return pl.pallas_call(
        cut_kernel,
        in_specs=[SMEM, ANY, ANY],
        out_specs=ANY,
        out_shape=jax.ShapeDtypeStruct((2, first.shape[1], width), first.dtype),
        scratch_shapes=[pltpu.SemaphoreType.DMA((2,))],
        compiler_params=pltpu.CompilerParams(vmem_limit_bytes=VMEM_LIMIT),
        name="cut_piece",
    )(place, first, second)


def prepare_kernel(
    lengths, x, g, xv, gv, down_t, up, columns, rows_t,
    top_out, bottom_out, proj_out,
    back, fwd, vback, vfwd, xc, gc,
):
    step = pl.program_id(0)

    @pl.when(step == 0)
    def _():
        for total in (back, fwd, vback, vfwd, xc, gc):
            total[...] = jnp.zeros_like(total)

    k2 = columns.shape[1]
    table = jnp.concatenate(two_terms(columns[...]), axis=1)
    back[...] += mm(g[...], up[...], NT)
    fwd[...] += mm(x[...], down_t[...], NT)
    vback[...] += mm(gv[...], up[...], NT)
    vfwd[...] += mm(xv[...], down_t[...], NT)
    xc[...] += mm(xv[...], table)
    gc[...] += mm(gv[...], table)

    @pl.when(step == pl.num_programs(0) - 1)
    def _():
        tokens, rank = back.shape
        position = lax.broadcasted_iota(jnp.int32, (rank, tokens), 1)
        back_t = back[...].T
        fwd_t = fwd[...].T
        begin = jnp.int32(0)
        for e in range(lengths.shape[0]):
            finish = begin + lengths[e]
            member = (position >= begin) & (position < finish)
            top_out[pl.ds(e * rank, rank), :] = jnp.where(member, back_t, 0.0).astype(jnp.bfloat16)
            bottom_out[pl.ds(e * rank, rank), :] = jnp.where(member, fwd_t, 0.0).astype(jnp.bfloat16)
            begin = finish
        round_b = vback[...].astype(jnp.bfloat16).astype(jnp.float32)
        round_f = vfwd[...].astype(jnp.bfloat16).astype(jnp.float32)
        inner_top = mm(round_b, xc[:, :k2] + xc[:, k2:], TN, HIGHEST)
        inner_bottom = mm(round_f, gc[:, :k2] + gc[:, k2:], TN, HIGHEST)
        inner = jnp.concatenate([inner_top, inner_bottom], axis=0)
        proj_out[...] = mm(rows_t[...], inner, NN, HIGHEST)


def prepare(lengths, x, g, xv, gv, down_t, up, columns, rows_t):
    tokens, width = x.shape
    val_tokens = xv.shape[0]
    rank = up.shape[0]
    k1, k2 = rows_t.shape[0], columns.shape[1]
    examples = lengths.shape[0]
    span = 1024
    whole = lambda i: (0, 0)
    across = lambda i: (0, i)
    along = lambda i: (i, 0)
    return pl.pallas_call(
        prepare_kernel,
        grid=(width // span,),
        in_specs=[
            SMEM,
            pl.BlockSpec((tokens, span), across),
            pl.BlockSpec((tokens, span), across),
            pl.BlockSpec((val_tokens, span), across),
            pl.BlockSpec((val_tokens, span), across),
            pl.BlockSpec((rank, span), across),
            pl.BlockSpec((rank, span), across),
            pl.BlockSpec((span, k2), along),
            pl.BlockSpec(rows_t.shape, whole),
        ],
        out_specs=[
            pl.BlockSpec((examples * rank, tokens), whole),
            pl.BlockSpec((examples * rank, tokens), whole),
            pl.BlockSpec((k1, k2), whole),
        ],
        out_shape=[
            jax.ShapeDtypeStruct((examples * rank, tokens), jnp.bfloat16),
            jax.ShapeDtypeStruct((examples * rank, tokens), jnp.bfloat16),
            jax.ShapeDtypeStruct((k1, k2), jnp.float32),
        ],
        scratch_shapes=[
            pltpu.VMEM((tokens, rank), jnp.float32),
            pltpu.VMEM((tokens, rank), jnp.float32),
            pltpu.VMEM((val_tokens, rank), jnp.float32),
            pltpu.VMEM((val_tokens, rank), jnp.float32),
            pltpu.VMEM((val_tokens, 2 * k2), jnp.float32),
            pltpu.VMEM((val_tokens, 2 * k2), jnp.float32),
        ],
        compiler_params=pltpu.CompilerParams(vmem_limit_bytes=VMEM_LIMIT),
        cost_estimate=pl.CostEstimate(
            flops=4 * tokens * width * rank, bytes_accessed=12_000_000, transcendentals=0
        ),
        name="prepare",
    )(lengths, x, g, xv, gv, down_t, up, columns, rows_t)


def piece_copies(ids, moment_refs, x, g, columns, xs, gs, cs, ms, sems, width):
    copies = []
    for i, (first, second) in enumerate(moment_refs(width)):
        at = pl.multiple_of(ids[i] * width, width)
        cols = pl.ds(at, width)
        copies.append(
            [
                pltpu.make_async_copy(first, ms.at[i, 0], sems.at[i, 0]),
                pltpu.make_async_copy(second, ms.at[i, 1], sems.at[i, 1]),
                pltpu.make_async_copy(x.at[:, cols], xs.at[i], sems.at[i, 2]),
                pltpu.make_async_copy(g.at[:, cols], gs.at[i], sems.at[i, 3]),
                pltpu.make_async_copy(columns.at[cols, :], cs.at[i], sems.at[i, 4]),
            ]
        )
    return copies


def accumulate(ids, moment_refs, x, g, columns, top, bottom, xs, gs, cs, ms, update, inner, sems):
    count, _, width = xs.shape
    rank = ms.shape[2] // 2
    examples = top.shape[0] // rank
    copies = piece_copies(ids, moment_refs, x, g, columns, xs, gs, cs, ms, sems, width)
    for piece in copies:
        for copy in piece:
            copy.start()
    inner[...] = jnp.zeros_like(inner)

    @pl.loop(0, count, step=2)
    def _(i):
        for j in (0, 1):
            for copy in (
                pltpu.make_async_copy(x.at[:, pl.ds(0, width)], xs.at[i + j], sems.at[i + j, 2]),
                pltpu.make_async_copy(g.at[:, pl.ds(0, width)], gs.at[i + j], sems.at[i + j, 3]),
                pltpu.make_async_copy(columns.at[pl.ds(0, width), :], cs.at[i + j], sems.at[i + j, 4]),
                pltpu.make_async_copy(ms.at[0, 0], ms.at[i + j, 0], sems.at[i + j, 0]),
                pltpu.make_async_copy(ms.at[0, 1], ms.at[i + j, 1], sems.at[i + j, 1]),
            ):
                copy.wait()
        terms = [two_terms(cs[i + j]) for j in (0, 1)]
        table = jnp.concatenate(
            [jnp.concatenate([terms[0][k], terms[1][k]], axis=0) for k in (0, 1)], axis=1
        )
        for half, (source, masked) in enumerate(((xs, top), (gs, bottom))):
            for j in (0, 1):
                cols = pl.ds(j * width, width)
                part = pl.ds(half * rank, rank)
                grad = mm(masked[...], source[i + j])
                first = 9.0 * ms[i + j, 0, part, :].astype(jnp.float32)
                second = 999.0 * ms[i + j, 1, part, :].astype(jnp.float32)
                shared = first * lax.rsqrt(second)
                coarse, fine = two_terms(shared)
                update[half, pl.ds(examples * rank, rank), cols] = coarse
                update[half, pl.ds((examples + 1) * rank, rank), cols] = fine
                for e in range(examples):
                    piece = grad[e * rank : (e + 1) * rank]
                    change = (first + piece) * lax.rsqrt(second + piece * piece) - shared
                    update[half, pl.ds(e * rank, rank), cols] = change.astype(jnp.bfloat16)
            inner[half] += mm(update[half], table)


def folded(inner, half, examples, rank, e):
    k2 = inner.shape[2] // 2
    part = pl.ds(e * rank, rank)
    total = inner[half, part, :k2] + inner[half, part, k2:]
    if e == examples:
        part = pl.ds((examples + 1) * rank, rank)
        total = total + inner[half, part, :k2] + inner[half, part, k2:]
    return total


def chunk_kernel(refs_of, n_moments, ids, *refs):
    moments, refs = refs[:n_moments], refs[n_moments:]
    x, g, columns, top, bottom, out, xs, gs, cs, ms, update, inner, sems = refs
    accumulate(
        ids, functools.partial(refs_of, moments), x, g, columns, top, bottom, xs, gs, cs, ms, update, inner, sems
    )
    rank = ms.shape[2] // 2
    examples = top.shape[0] // rank
    for half in (0, 1):
        for e in range(examples + 1):
            out[half, pl.ds(e * rank, rank), :] = folded(inner, half, examples, rank, e)


def last_kernel(refs_of, n_moments, n_partial, ids, *refs):
    moments, refs = refs[:n_moments], refs[n_moments:]
    x, g, columns, top, bottom, rows_t = refs[:6]
    val_parts, refs = refs[6:8], refs[8:]
    partials, refs = refs[:n_partial], refs[n_partial:]
    dirs_out, val_out, scores_out, joined, xs, gs, cs, ms, update, inner, sems = refs
    accumulate(
        ids, functools.partial(refs_of, moments), x, g, columns, top, bottom, xs, gs, cs, ms, update, inner, sems
    )
    rank = ms.shape[2] // 2
    examples = top.shape[0] // rank
    size = rows_t.shape[0] * columns.shape[1]
    val = val_parts[0][...] + val_parts[1][...]
    val_dir = val * lax.rsqrt(jnp.sum(val * val) / size + epsilon)
    val_out[...] = val_dir
    rows = rows_t[...] * update_scale

    k2 = columns.shape[1]
    for e in range(examples + 1):
        for half in (0, 1):
            total = folded(inner, half, examples, rank, e)
            for partial in partials:
                total = total + partial[half, pl.ds(e * rank, rank), :]
            joined[pl.ds(half * rank, rank), pl.ds(e * k2, k2)] = total
    projected = mm(rows, joined[...], NN, HIGHEST)
    base = projected[:, examples * k2 :]
    for e in range(examples):
        proj = projected[:, e * k2 : (e + 1) * k2] + base
        direction = proj * lax.rsqrt(jnp.sum(proj * proj) / size + epsilon)
        dirs_out[e] = direction
        scores_out[e] = jnp.sum(direction * val_dir) / math.sqrt(size)


def chunk(ids, moments, refs_of, width, x, g, columns, top, bottom, last=None):
    count = ids.shape[0]
    tokens = x.shape[0]
    k2 = columns.shape[1]
    rank2 = moments[0].shape[-2]
    rank = rank2 // 2
    examples = top.shape[0] // rank
    scratch = [
        pltpu.VMEM((count, tokens, width), jnp.bfloat16),
        pltpu.VMEM((count, tokens, width), jnp.bfloat16),
        pltpu.VMEM((count, width, k2), jnp.float32),
        pltpu.VMEM((count, 2, rank2, width), jnp.bfloat16),
        pltpu.VMEM((2, (examples + 2) * rank, 2 * width), jnp.bfloat16),
        pltpu.VMEM((2, (examples + 2) * rank, 2 * k2), jnp.float32),
        pltpu.SemaphoreType.DMA((count, 5)),
    ]
    vmem = pl.BlockSpec(memory_space=pltpu.VMEM)
    cost = pl.CostEstimate(
        flops=4 * tokens * width * count * rank * examples,
        bytes_accessed=400_000 * count,
        transcendentals=0,
    )
    common = [SMEM] + [ANY] * len(moments) + [ANY, ANY, ANY, vmem, vmem]
    operands = [ids, *moments, x, g, columns, top, bottom]
    params = pltpu.CompilerParams(vmem_limit_bytes=VMEM_LIMIT)
    if last is None:
        return pl.pallas_call(
            functools.partial(chunk_kernel, refs_of, len(moments)),
            in_specs=common,
            out_specs=vmem,
            out_shape=jax.ShapeDtypeStruct((2, (examples + 1) * rank, k2), jnp.float32),
            scratch_shapes=scratch,
            compiler_params=params,
            cost_estimate=cost,
            name="chunk",
        )(*operands)
    rows_t, val_parts, partials = last
    k1 = rows_t.shape[0]
    return pl.pallas_call(
        functools.partial(last_kernel, refs_of, len(moments), len(partials)),
        in_specs=common + [vmem] * (3 + len(partials)),
        out_specs=[vmem, vmem, SMEM],
        out_shape=[
            jax.ShapeDtypeStruct((examples, k1, k2), jnp.float32),
            jax.ShapeDtypeStruct((k1, k2), jnp.float32),
            jax.ShapeDtypeStruct((examples,), jnp.float32),
        ],
        scratch_shapes=[pltpu.VMEM((rank2, (examples + 1) * k2), jnp.float32), *scratch],
        compiler_params=params,
        cost_estimate=cost,
        name="last_chunk",
    )(*operands, rows_t, *val_parts, *partials)


def refs_of_pieces(moments, width):
    return [(piece.at[0], piece.at[1]) for piece in moments]


def refs_of_blocks(moments, width):
    found = []
    for first, second in zip(moments[::2], moments[1::2]):
        for at in range(0, first.shape[2], width):
            cols = pl.ds(at, width)
            found.append((first.at[0, :, cols], second.at[0, :, cols]))
    return found


def refs_of_gathered(moments, width):
    return [(moments[0].at[b], moments[1].at[b]) for b in range(moments[0].shape[0])]


def exchange(value, axis, bits):
    size = lax.axis_size(axis)
    return lax.ppermute(value, axis, [(i, i ^ bits) for i in range(size)])


def body(
    training_inputs,
    training_cotangents,
    validation_inputs,
    validation_cotangents,
    adapter_down,
    adapter_up,
    adam_first_moment,
    adam_second_moment,
    slot_block_index,
    example_lengths,
    projection_rows,
    projection_columns,
):
    groups = lax.axis_size("dp")
    shards = lax.axis_size("shard")
    block_width = adam_first_moment.shape[2]
    width = block_width // groups
    stepwise = groups == 4 and shards == 8 and width % 128 == 0
    group = lax.axis_index("dp").astype(jnp.int32)
    shard = lax.axis_index("shard").astype(jnp.int32)
    rows_t = projection_rows.T
    prepared = prepare(
        example_lengths[0, 0],
        training_inputs,
        training_cotangents,
        validation_inputs,
        validation_cotangents,
        adapter_down.T,
        adapter_up,
        projection_columns,
        rows_t,
    )
    top, bottom, val_part = prepared
    operands = (training_inputs, training_cotangents, projection_columns, top, bottom)
    if stepwise:
        own = cut_piece(group[None], adam_first_moment, adam_second_moment, width)
        sibling = [exchange(m, "shard", 1) for m in (adam_first_moment, adam_second_moment)]
        pieces = []
        for hop in (1, 2, 3):
            far = exchange(own, "shard", 2 * hop)
            four = [far] + [exchange(far, "dp", bits) for bits in (1, 2, 3)]
            pieces.append(four + [exchange(piece, "shard", 1) for piece in four])
        total = val_part
        for axis, unit in (("dp", 1), ("shard", 2)):
            others = [exchange(total, axis, unit * bits) for bits in (1, 2, 3)]
            total = (total + others[0]) + (others[1] + others[2])
        val_parts = [total, exchange(total, "shard", 1)]

        quarters = jnp.arange(groups, dtype=jnp.int32)

        def ids_of(hop, order):
            blocks = jnp.stack([slot_block_index[shard ^ (2 * hop)], slot_block_index[shard ^ (2 * hop) ^ 1]])
            return (blocks[:, None] * groups + order[None, :]).reshape(-1)

        partials = [
            chunk(
                ids_of(0, quarters),
                [adam_first_moment, adam_second_moment, *sibling],
                refs_of_blocks,
                width,
                *operands,
            )
        ]
        for hop in (1, 2):
            partials.append(chunk(ids_of(hop, group ^ quarters), pieces[hop - 1], refs_of_pieces, width, *operands))
        dirs, val_dir, scores = chunk(
            ids_of(3, group ^ quarters),
            pieces[2],
            refs_of_pieces,
            width,
            *operands,
            last=(rows_t, val_parts, partials),
        )
    else:
        gathered = [
            lax.all_gather(m, "shard", axis=0, tiled=True) for m in (adam_first_moment, adam_second_moment)
        ]
        val_sum = lax.psum(val_part, ("dp", "shard"))
        dirs, val_dir, scores = chunk(
            slot_block_index,
            gathered,
            refs_of_gathered,
            block_width,
            *operands,
            last=(rows_t, [val_sum, jnp.zeros_like(val_sum)], []),
        )
    return (
        dirs.reshape(1, 1, dirs.shape[0], -1),
        val_dir.reshape(-1),
        scores[None, None],
    )


def solution(mesh):
    return jax.shard_map(
        body,
        mesh=mesh,
        in_specs=(
            P(("dp", "shard"), None),
            P(("dp", "shard"), None),
            P(("dp", "shard"), None),
            P(("dp", "shard"), None),
            P(),
            P(),
            P("shard", None, None),
            P("shard", None, None),
            P(),
            P("dp", "shard", None),
            P(),
            P(),
        ),
        out_specs=(P("dp", "shard", None, None), P(), P("dp", "shard", None)),
        check_vma=False,
    )
```

```python
import functools
import math

import jax
import jax.numpy as jnp
from jax import lax
from jax.experimental import pallas as pl
from jax.experimental.pallas import tpu as pltpu
from jax.sharding import PartitionSpec as P

epsilon = 1e-06
update_scale = 0.1 / math.sqrt(0.001)
HIGHEST = lax.Precision.HIGHEST
NN = (((1,), (0,)), ((), ()))
TN = (((0,), (0,)), ((), ()))
NT = (((1,), (1,)), ((), ()))
VMEM_LIMIT = 60 * 1024 * 1024
CHUNK_LIMIT = 24 * 1024 * 1024
ANY = pl.BlockSpec(memory_space=pl.ANY)
SMEM = pl.BlockSpec(memory_space=pltpu.SMEM)
VMEM = pl.BlockSpec(memory_space=pltpu.VMEM)


def mm(a, b, dims=NN, precision=None):
    return lax.dot_general(a, b, dims, precision=precision, preferred_element_type=jnp.float32)


def two_terms(exact):
    coarse = exact.astype(jnp.bfloat16)
    fine = (exact - coarse.astype(jnp.float32)).astype(jnp.bfloat16)
    return coarse, fine


def cut_kernel(first, second, out, sems):
    group = lax.axis_index("dp")
    copies = [
        pltpu.make_async_copy(source.at[group], out.at[i], sems.at[i])
        for i, source in enumerate((first, second))
    ]
    for copy in copies:
        copy.start()
    for copy in copies:
        copy.wait()


def cut_piece(first, second):
    return pl.pallas_call(
        cut_kernel,
        in_specs=[ANY, ANY],
        out_specs=VMEM,
        out_shape=jax.ShapeDtypeStruct((2,) + first.shape[1:], first.dtype),
        scratch_shapes=[pltpu.SemaphoreType.DMA((2,))],
        compiler_params=pltpu.CompilerParams(vmem_limit_bytes=VMEM_LIMIT),
        name="cut_piece",
    )(first, second)


def prepare_kernel(
    span, lengths, x, g, xv, gv, down_t, up, columns, rows_t,
    top_out, bottom_out, proj_out,
    xs, gs, xvs, gvs, downs, ups, tables, sems,
):
    width = x.shape[1]
    steps = width // span
    copies = []
    for i in range(steps):
        cols = pl.ds(i * span, span)
        pairs = [(up, ups), (g, gs), (down_t, downs), (x, xs), (xv, xvs), (gv, gvs)]
        step = [
            pltpu.make_async_copy(source.at[:, cols], target.at[:, cols], sems.at[i, k])
            for k, (source, target) in enumerate(pairs)
        ]
        step.append(pltpu.make_async_copy(columns.at[cols, :], tables.at[cols, :], sems.at[i, len(pairs)]))
        copies.append(step)
    for step in copies:
        for copy in step:
            copy.start()
    back = fwd = vback = vfwd = xc = gc = 0.0
    k2 = columns.shape[1]
    for i in range(steps):
        for copy in copies[i]:
            copy.wait()
        cols = pl.ds(i * span, span)
        table = jnp.concatenate(two_terms(tables[cols, :]), axis=1)
        back = back + mm(gs[:, cols], ups[:, cols], NT)
        fwd = fwd + mm(xs[:, cols], downs[:, cols], NT)
        vback = vback + mm(gvs[:, cols], ups[:, cols], NT)
        vfwd = vfwd + mm(xvs[:, cols], downs[:, cols], NT)
        xc = xc + mm(xvs[:, cols], table)
        gc = gc + mm(gvs[:, cols], table)
    tokens, rank = back.shape
    position = lax.broadcasted_iota(jnp.int32, (rank, tokens), 1)
    back_t = back.T
    fwd_t = fwd.T
    begin = jnp.int32(0)
    for e in range(lengths.shape[0]):
        finish = begin + lengths[e]
        member = (position >= begin) & (position < finish)
        top_out[pl.ds(e * rank, rank), :] = jnp.where(member, back_t, 0.0).astype(jnp.bfloat16)
        bottom_out[pl.ds(e * rank, rank), :] = jnp.where(member, fwd_t, 0.0).astype(jnp.bfloat16)
        begin = finish
    round_b = vback.astype(jnp.bfloat16).astype(jnp.float32)
    round_f = vfwd.astype(jnp.bfloat16).astype(jnp.float32)
    inner_top = mm(round_b, xc[:, :k2] + xc[:, k2:], TN, HIGHEST)
    inner_bottom = mm(round_f, gc[:, :k2] + gc[:, k2:], TN, HIGHEST)
    inner = jnp.concatenate([inner_top, inner_bottom], axis=0)
    proj_out[...] = mm(rows_t[...], inner, NN, HIGHEST)


def prepare(lengths, x, g, xv, gv, down_t, up, columns, rows_t):
    tokens, width = x.shape
    rank = up.shape[0]
    k1, k2 = rows_t.shape[0], columns.shape[1]
    examples = lengths.shape[0]
    span = 2048
    return pl.pallas_call(
        functools.partial(prepare_kernel, span),
        in_specs=[SMEM] + [ANY] * 7 + [VMEM],
        out_specs=[VMEM] * 3,
        out_shape=[
            jax.ShapeDtypeStruct((examples * rank, tokens), jnp.bfloat16),
            jax.ShapeDtypeStruct((examples * rank, tokens), jnp.bfloat16),
            jax.ShapeDtypeStruct((k1, k2), jnp.float32),
        ],
        scratch_shapes=[
            *(pltpu.VMEM(a.shape, a.dtype) for a in (x, g, xv, gv, down_t, up, columns)),
            pltpu.SemaphoreType.DMA((width // span, 7)),
        ],
        compiler_params=pltpu.CompilerParams(vmem_limit_bytes=VMEM_LIMIT),
        cost_estimate=pl.CostEstimate(
            flops=4 * tokens * width * rank, bytes_accessed=20_000_000, transcendentals=0
        ),
        name="prepare",
    )(lengths, x, g, xv, gv, down_t, up, columns, rows_t)


def accumulate(block_of, copies_of, moments, slots, x, g, columns, top, bottom, xs, gs, cs, ms, update, inner, sems):
    count, _, span = xs.shape
    rank = ms.shape[1] * ms.shape[3] // 2
    examples = top.shape[0] // rank
    copies = []
    for b in range(count):
        cols = pl.ds(pl.multiple_of(slots[block_of(b)] * span, span), span)
        pairs = [(x.at[:, cols], xs.at[b]), (g.at[:, cols], gs.at[b]), (columns.at[cols, :], cs.at[b])]
        pairs += copies_of(moments, b, ms.at[b])
        copies.append([pltpu.make_async_copy(p[0], p[1], sems.at[b, k]) for k, p in enumerate(pairs)])
    for block in copies:
        for copy in block:
            copy.start()
    inner[...] = jnp.zeros_like(inner)
    cut = min(span, 256)
    half_parts = ms.shape[1] // 2
    for b in range(count):
        for copy in copies[b]:
            copy.wait()
        table = jnp.concatenate(two_terms(cs[b]), axis=1)
        for half, (source, masked) in enumerate(((xs, top), (gs, bottom))):
            parts = slice(half * half_parts, (half + 1) * half_parts)
            for c in range(0, span, cut):
                cols = pl.ds(c, cut)
                grad = mm(masked[...], source[b, :, cols])
                first = 9.0 * ms[b, parts, 0, :, cols].astype(jnp.float32).reshape(rank, cut)
                second = 999.0 * ms[b, parts, 1, :, cols].astype(jnp.float32).reshape(rank, cut)
                shared = first * lax.rsqrt(second)
                coarse, fine = two_terms(shared)
                update[half, pl.ds(examples * rank, rank), cols] = coarse
                update[half, pl.ds((examples + 1) * rank, rank), cols] = fine
                for e in range(examples):
                    piece = grad[e * rank : (e + 1) * rank]
                    change = (first + piece) * lax.rsqrt(second + piece * piece) - shared
                    update[half, pl.ds(e * rank, rank), cols] = change.astype(jnp.bfloat16)
            inner[half] += mm(update[half], table)


def folded(inner, half, examples, rank, e):
    k2 = inner.shape[2] // 2
    part = pl.ds(e * rank, rank)
    total = inner[half, part, :k2] + inner[half, part, k2:]
    if e == examples:
        part = pl.ds((examples + 1) * rank, rank)
        total = total + inner[half, part, :k2] + inner[half, part, k2:]
    return total


def chunk_kernel(block_of, copies_of, n_moments, slots, *refs):
    moments, refs = refs[:n_moments], refs[n_moments:]
    x, g, columns, top, bottom, out, xs, gs, cs, ms, update, inner, sems = refs
    accumulate(
        block_of, copies_of, moments, slots, x, g, columns, top, bottom, xs, gs, cs, ms, update, inner, sems
    )
    rank = ms.shape[1] * ms.shape[3] // 2
    examples = top.shape[0] // rank
    for half in (0, 1):
        for e in range(examples + 1):
            out[half, pl.ds(e * rank, rank), :] = folded(inner, half, examples, rank, e)


def last_kernel(block_of, copies_of, n_moments, n_partial, slots, *refs):
    moments, refs = refs[:n_moments], refs[n_moments:]
    x, g, columns, top, bottom, rows_t = refs[:6]
    val_parts, refs = refs[6:8], refs[8:]
    partials, refs = refs[:n_partial], refs[n_partial:]
    dirs_out, val_out, scores_out, joined, xs, gs, cs, ms, update, inner, sems = refs
    accumulate(
        block_of, copies_of, moments, slots, x, g, columns, top, bottom, xs, gs, cs, ms, update, inner, sems
    )
    rank = ms.shape[1] * ms.shape[3] // 2
    examples = top.shape[0] // rank
    k1, k2 = rows_t.shape[0], columns.shape[1]
    size = k1 * k2
    val = val_parts[0][...] + val_parts[1][...]
    val_dir = val * lax.rsqrt(jnp.sum(val * val) / size + epsilon)
    val_out[...] = val_dir
    rows = rows_t[...] * update_scale
    for e in range(examples + 1):
        for half in (0, 1):
            total = folded(inner, half, examples, rank, e)
            for partial in partials:
                total = total + partial[half, pl.ds(e * rank, rank), :]
            joined[pl.ds(half * rank, rank), pl.ds(e * k2, k2)] = total
    projected = mm(rows, joined[...], NN, HIGHEST)
    base = projected[:, examples * k2 :]
    for e in range(examples):
        proj = projected[:, e * k2 : (e + 1) * k2] + base
        direction = proj * lax.rsqrt(jnp.sum(proj * proj) / size + epsilon)
        dirs_out[e] = direction
        scores_out[e] = jnp.sum(direction * val_dir) / math.sqrt(size)


def chunk(slots, count, block_of, copies_of, n_copies, parts, moments, x, g, columns, top, bottom, last=None):
    tokens, width = x.shape
    k2 = columns.shape[1]
    span = width // slots.shape[0]
    quarter, rank = parts
    pieces = 2 * rank // quarter
    examples = top.shape[0] // rank
    scratch = [
        pltpu.VMEM((count, tokens, span), jnp.bfloat16),
        pltpu.VMEM((count, tokens, span), jnp.bfloat16),
        pltpu.VMEM((count, span, k2), jnp.float32),
        pltpu.VMEM((count, pieces, 2, quarter, span), jnp.bfloat16),
        pltpu.VMEM((2, (examples + 2) * rank, span), jnp.bfloat16),
        pltpu.VMEM((2, (examples + 2) * rank, 2 * k2), jnp.float32),
        pltpu.SemaphoreType.DMA((count, 3 + n_copies)),
    ]
    cost = pl.CostEstimate(
        flops=4 * tokens * span * count * rank * examples,
        bytes_accessed=6_000_000 * count,
        transcendentals=0,
    )
    common = [SMEM] + [ANY] * len(moments) + [ANY, ANY, ANY, VMEM, VMEM]
    operands = [slots, *moments, x, g, columns, top, bottom]
    params = pltpu.CompilerParams(vmem_limit_bytes=CHUNK_LIMIT)
    if last is None:
        return pl.pallas_call(
            functools.partial(chunk_kernel, block_of, copies_of, len(moments)),
            in_specs=common,
            out_specs=VMEM,
            out_shape=jax.ShapeDtypeStruct((2, (examples + 1) * rank, k2), jnp.float32),
            scratch_shapes=scratch,
            compiler_params=params,
            cost_estimate=cost,
            name="chunk",
        )(*operands)
    rows_t, val_parts, partials = last
    k1 = rows_t.shape[0]
    return pl.pallas_call(
        functools.partial(last_kernel, block_of, copies_of, len(moments), len(partials)),
        in_specs=common + [VMEM] * (3 + len(partials)),
        out_specs=[VMEM, VMEM, SMEM],
        out_shape=[
            jax.ShapeDtypeStruct((examples, k1, k2), jnp.float32),
            jax.ShapeDtypeStruct((k1, k2), jnp.float32),
            jax.ShapeDtypeStruct((examples,), jnp.float32),
        ],
        scratch_shapes=[pltpu.VMEM((2 * rank, (examples + 1) * k2), jnp.float32), *scratch],
        compiler_params=params,
        cost_estimate=cost,
        name="last_chunk",
    )(*operands, rows_t, *val_parts, *partials)


def copies_of_pieces(moments, b, target):
    group = lax.axis_index("dp")
    return [(piece.at[b], target.at[lax.bitwise_xor(group, j)]) for j, piece in enumerate(moments)]


def copies_of_blocks(moments, b, target):
    return [(moments[2 * b + k], target.at[:, k]) for k in (0, 1)]


def copies_of_gathered(moments, b, target):
    return [(moments[k].at[b], target.at[:, k]) for k in (0, 1)]


def slot_at(other, hop):
    return lax.bitwise_xor(lax.axis_index("shard"), 2 * hop + other)


def exchange(value, axis, bits):
    size = lax.axis_size(axis)
    return lax.ppermute(value, axis, [(i, i ^ bits) for i in range(size)])


def spread_sum(own, others):
    return (own + others[0]) + (others[1] + others[2])


def body(
    training_inputs,
    training_cotangents,
    validation_inputs,
    validation_cotangents,
    adapter_down,
    adapter_up,
    adam_first_moment,
    adam_second_moment,
    slot_block_index,
    example_lengths,
    projection_rows,
    projection_columns,
):
    groups = lax.axis_size("dp")
    shards = lax.axis_size("shard")
    rank = adapter_up.shape[0]
    quarter = 2 * rank // groups
    parts = (quarter, rank)
    stepwise = groups == 4 and shards == 8
    rows_t = projection_rows.T
    own = [m.reshape(groups, quarter, -1) for m in (adam_first_moment, adam_second_moment)]
    train = (training_inputs, training_cotangents)
    if stepwise:
        piece = cut_piece(*own)
        sibling = [exchange(m, "shard", 1) for m in own]
        far = [exchange(piece, "shard", 2 * hop) for hop in (1, 2, 3)]
    top, bottom, val_part = prepare(
        example_lengths[0, 0],
        *train,
        validation_inputs,
        validation_cotangents,
        adapter_down.T,
        adapter_up,
        projection_columns,
        rows_t,
    )
    if stepwise:
        *arrived, top, bottom, val_part = lax.optimization_barrier((*far, *sibling, top, bottom, val_part))
        far, sibling = jnp.stack(arrived[:3]), arrived[3:]
        four = [far] + [exchange(far, "dp", bits) for bits in (1, 2, 3)]
        total = spread_sum(val_part, [exchange(val_part, "dp", bits) for bits in (1, 2, 3)])
        total, top, bottom = lax.optimization_barrier((total, top, bottom))
        others = [exchange(total, "shard", 2 * bits) for bits in (1, 2, 3)]
        operands = (*train, projection_columns, top, bottom)
        first = chunk(
            slot_block_index, 2, lambda b: slot_at(b, 0), copies_of_blocks, 2, parts, own + sibling, *operands
        )
        first, *arrived = lax.optimization_barrier((first, *others, *four))
        total = spread_sum(total, arrived[:3])
        val_parts = [total, exchange(total, "shard", 1)]
        four = arrived[3:]
        crossed = [exchange(part, "shard", 1) for part in four]
        second = chunk(
            slot_block_index, 3, lambda b: slot_at(0, b + 1), copies_of_pieces, 4, parts, four, *operands
        )
        partials = [first, second]
        dirs, val_dir, scores = chunk(
            slot_block_index,
            3,
            lambda b: slot_at(1, b + 1),
            copies_of_pieces,
            4,
            parts,
            crossed,
            *operands,
            last=(rows_t, val_parts, partials),
        )
    else:
        operands = (*train, projection_columns, top, bottom)
        gathered = [lax.all_gather(m, "shard", axis=0, tiled=False) for m in own]
        val_sum = lax.psum(val_part, ("dp", "shard"))
        dirs, val_dir, scores = chunk(
            slot_block_index,
            shards,
            lambda b: b,
            copies_of_gathered,
            2,
            parts,
            gathered,
            *operands,
            last=(rows_t, [val_sum, jnp.zeros_like(val_sum)], []),
        )
    return (
        dirs.reshape(1, 1, dirs.shape[0], -1),
        val_dir.reshape(-1),
        scores[None, None],
    )


def solution(mesh):
    return jax.shard_map(
        body,
        mesh=mesh,
        in_specs=(
            P(("dp", "shard"), None),
            P(("dp", "shard"), None),
            P(("dp", "shard"), None),
            P(("dp", "shard"), None),
            P(),
            P(),
            P("shard", None, None),
            P("shard", None, None),
            P(),
            P("dp", "shard", None),
            P(),
            P(),
        ),
        out_specs=(P("dp", "shard", None, None), P(), P("dp", "shard", None)),
        check_vma=False,
    )
```

```python
import functools
import math

import jax
import jax.numpy as jnp
from jax import lax
from jax.experimental import pallas as pl
from jax.experimental.pallas import tpu as pltpu
from jax.sharding import PartitionSpec as P

epsilon = 1e-06
update_scale = 0.1 / math.sqrt(0.001)
HIGHEST = lax.Precision.HIGHEST
NN = (((1,), (0,)), ((), ()))
TN = (((0,), (0,)), ((), ()))
NT = (((1,), (1,)), ((), ()))
VMEM_LIMIT = 60 * 1024 * 1024
CHUNK_LIMIT = 24 * 1024 * 1024
ANY = pl.BlockSpec(memory_space=pl.ANY)
SMEM = pl.BlockSpec(memory_space=pltpu.SMEM)
VMEM = pl.BlockSpec(memory_space=pltpu.VMEM)


def mm(a, b, dims=NN, precision=None):
    return lax.dot_general(a, b, dims, precision=precision, preferred_element_type=jnp.float32)


def two_terms(exact):
    coarse = exact.astype(jnp.bfloat16)
    fine = (exact - coarse.astype(jnp.float32)).astype(jnp.bfloat16)
    return coarse, fine


def cut_kernel(first, second, out, sems):
    group = lax.axis_index("dp")
    copies = [
        pltpu.make_async_copy(source.at[group], out.at[i], sems.at[i])
        for i, source in enumerate((first, second))
    ]
    for copy in copies:
        copy.start()
    for copy in copies:
        copy.wait()


def cut_piece(first, second):
    return pl.pallas_call(
        cut_kernel,
        in_specs=[ANY, ANY],
        out_specs=VMEM,
        out_shape=jax.ShapeDtypeStruct((2,) + first.shape[1:], first.dtype),
        scratch_shapes=[pltpu.SemaphoreType.DMA((2,))],
        compiler_params=pltpu.CompilerParams(vmem_limit_bytes=VMEM_LIMIT),
        name="cut_piece",
    )(first, second)


def load(pairs, sems):
    steps = sems.shape[0]
    copies = []
    for i in range(steps):
        step = []
        for k, (source, target, axis) in enumerate(pairs):
            span = source.shape[axis] // steps
            at = (slice(None),) * axis + (pl.ds(i * span, span),)
            step.append(pltpu.make_async_copy(source.at[at], target.at[at], sems.at[i, k]))
        copies.append(step)
    for step in copies:
        for copy in step:
            copy.start()
    return copies


def validation_kernel(xv, gv, down_t, up, columns, rows_t, proj_out, xvs, gvs, downs, ups, tables, sems):
    pairs = [(xv, xvs, 1), (gv, gvs, 1), (up, ups, 1), (down_t, downs, 1), (columns, tables, 0)]
    copies = load(pairs, sems)
    steps = len(copies)
    span = xv.shape[1] // steps
    tokens = xv.shape[0]
    k2 = columns.shape[1]
    back = fwd = mixed = 0.0
    for i in range(steps):
        for copy in copies[i]:
            copy.wait()
        cols = pl.ds(i * span, span)
        table = jnp.concatenate(two_terms(tables[cols, :]), axis=1)
        back = back + mm(gvs[:, cols], ups[:, cols], NT)
        fwd = fwd + mm(xvs[:, cols], downs[:, cols], NT)
        mixed = mixed + mm(jnp.concatenate([xvs[:, cols], gvs[:, cols]], axis=0), table)
    mixed = mixed[:, :k2] + mixed[:, k2:]
    inner_top = mm(back.astype(jnp.bfloat16).astype(jnp.float32), mixed[:tokens], TN, HIGHEST)
    inner_bottom = mm(fwd.astype(jnp.bfloat16).astype(jnp.float32), mixed[tokens:], TN, HIGHEST)
    inner = jnp.concatenate([inner_top, inner_bottom], axis=0)
    proj_out[...] = mm(rows_t[...], inner, NN, HIGHEST)


def prepare_kernel(lengths, x, g, down_t, up, top_out, bottom_out, xs, gs, downs, ups, sems):
    copies = load([(g, gs, 1), (up, ups, 1), (x, xs, 1), (down_t, downs, 1)], sems)
    steps = len(copies)
    span = x.shape[1] // steps
    back = fwd = 0.0
    for i in range(steps):
        for copy in copies[i]:
            copy.wait()
        cols = pl.ds(i * span, span)
        back = back + mm(gs[:, cols], ups[:, cols], NT)
        fwd = fwd + mm(xs[:, cols], downs[:, cols], NT)
    tokens, rank = back.shape
    position = lax.broadcasted_iota(jnp.int32, (rank, tokens), 1)
    back_t = back.T
    fwd_t = fwd.T
    begin = jnp.int32(0)
    for e in range(lengths.shape[0]):
        finish = begin + lengths[e]
        member = (position >= begin) & (position < finish)
        top_out[pl.ds(e * rank, rank), :] = jnp.where(member, back_t, 0.0).astype(jnp.bfloat16)
        bottom_out[pl.ds(e * rank, rank), :] = jnp.where(member, fwd_t, 0.0).astype(jnp.bfloat16)
        begin = finish


STEPS = 4


def validation(xv, gv, down_t, up, columns, rows_t):
    return pl.pallas_call(
        validation_kernel,
        in_specs=[ANY] * 5 + [VMEM],
        out_specs=VMEM,
        out_shape=jax.ShapeDtypeStruct((rows_t.shape[0], columns.shape[1]), jnp.float32),
        scratch_shapes=[
            *(pltpu.VMEM(a.shape, a.dtype) for a in (xv, gv, down_t, up, columns)),
            pltpu.SemaphoreType.DMA((STEPS, 5)),
        ],
        compiler_params=pltpu.CompilerParams(vmem_limit_bytes=VMEM_LIMIT),
        cost_estimate=pl.CostEstimate(flops=10**6, bytes_accessed=10**6, transcendentals=0),
        name="validation",
    )(xv, gv, down_t, up, columns, rows_t)


def prepare(lengths, x, g, down_t, up):
    shape = jax.ShapeDtypeStruct((lengths.shape[0] * up.shape[0], x.shape[0]), jnp.bfloat16)
    return pl.pallas_call(
        prepare_kernel,
        in_specs=[SMEM] + [ANY] * 4,
        out_specs=[VMEM] * 2,
        out_shape=[shape, shape],
        scratch_shapes=[
            *(pltpu.VMEM(a.shape, a.dtype) for a in (x, g, down_t, up)),
            pltpu.SemaphoreType.DMA((STEPS, 4)),
        ],
        compiler_params=pltpu.CompilerParams(vmem_limit_bytes=VMEM_LIMIT),
        cost_estimate=pl.CostEstimate(flops=10**6, bytes_accessed=10**6, transcendentals=0),
        name="prepare",
    )(lengths, x, g, down_t, up)


def accumulate(block_of, copies_of, moments, slots, x, g, columns, top, bottom, xs, gs, cs, ms, update, inner, sems):
    count, _, span = xs.shape
    rank = ms.shape[1] * ms.shape[3] // 2
    examples = top.shape[0] // rank
    copies = []
    for b in range(count):
        cols = pl.ds(pl.multiple_of(slots[block_of(b)] * span, span), span)
        pairs = [(x.at[:, cols], xs.at[b]), (g.at[:, cols], gs.at[b]), (columns.at[cols, :], cs.at[b])]
        pairs += copies_of(moments, b, ms.at[b])
        copies.append([pltpu.make_async_copy(p[0], p[1], sems.at[b, k]) for k, p in enumerate(pairs)])
    for copy in copies[0]:
        copy.start()
    inner[...] = jnp.zeros_like(inner)
    cut = min(span, 256)
    half_parts = ms.shape[1] // 2
    tiles = [(b, half, c) for b in range(count) for half in (0, 1) for c in range(0, span, cut)]
    sources, masks = (xs, gs), (top, bottom)

    def gradient(tile):
        b, half, c = tile
        if half == 0 and c == 0:
            for copy in copies[b]:
                copy.wait()
            if b + 1 < count:
                for copy in copies[b + 1]:
                    copy.start()
        return mm(masks[half][...], sources[half][b, :, pl.ds(c, cut)])

    def elementwise(tile, grad):
        b, half, c = tile
        cols = pl.ds(c, cut)
        parts = slice(half * half_parts, (half + 1) * half_parts)
        first = 9.0 * ms[b, parts, 0, :, cols].astype(jnp.float32).reshape(rank, cut)
        second = 999.0 * ms[b, parts, 1, :, cols].astype(jnp.float32).reshape(rank, cut)
        shared = first * lax.rsqrt(second)
        coarse, fine = two_terms(shared)
        update[half, pl.ds(examples * rank, rank), cols] = coarse
        update[half, pl.ds((examples + 1) * rank, rank), cols] = fine
        for e in range(examples):
            piece = grad[e * rank : (e + 1) * rank]
            change = (first + piece) * lax.rsqrt(second + piece * piece) - shared
            update[half, pl.ds(e * rank, rank), cols] = change.astype(jnp.bfloat16)

    grad = gradient(tiles[0])
    for i, tile in enumerate(tiles):
        following = gradient(tiles[i + 1]) if i + 1 < len(tiles) else None
        elementwise(tile, grad)
        grad = following
        b, half, c = tile
        if c + cut == span:
            table = jnp.concatenate(two_terms(cs[b]), axis=1)
            inner[half] += mm(update[half], table)


def folded(inner, half, examples, rank, e):
    k2 = inner.shape[2] // 2
    part = pl.ds(e * rank, rank)
    total = inner[half, part, :k2] + inner[half, part, k2:]
    if e == examples:
        part = pl.ds((examples + 1) * rank, rank)
        total = total + inner[half, part, :k2] + inner[half, part, k2:]
    return total


def chunk_kernel(block_of, copies_of, n_moments, slots, *refs):
    moments, refs = refs[:n_moments], refs[n_moments:]
    x, g, columns, top, bottom, out, xs, gs, cs, ms, update, inner, sems = refs
    accumulate(
        block_of, copies_of, moments, slots, x, g, columns, top, bottom, xs, gs, cs, ms, update, inner, sems
    )
    rank = ms.shape[1] * ms.shape[3] // 2
    examples = top.shape[0] // rank
    for half in (0, 1):
        for e in range(examples + 1):
            out[half, pl.ds(e * rank, rank), :] = folded(inner, half, examples, rank, e)


def last_kernel(block_of, copies_of, n_moments, n_partial, slots, *refs):
    moments, refs = refs[:n_moments], refs[n_moments:]
    x, g, columns, top, bottom, rows_t = refs[:6]
    val_parts, refs = refs[6:8], refs[8:]
    partials, refs = refs[:n_partial], refs[n_partial:]
    dirs_out, val_out, scores_out, joined, xs, gs, cs, ms, update, inner, sems = refs
    accumulate(
        block_of, copies_of, moments, slots, x, g, columns, top, bottom, xs, gs, cs, ms, update, inner, sems
    )
    rank = ms.shape[1] * ms.shape[3] // 2
    examples = top.shape[0] // rank
    k1, k2 = rows_t.shape[0], columns.shape[1]
    size = k1 * k2
    val = val_parts[0][...] + val_parts[1][...]
    val_dir = val * lax.rsqrt(jnp.sum(val * val) / size + epsilon)
    val_out[...] = val_dir
    rows = rows_t[...] * update_scale
    for e in range(examples + 1):
        for half in (0, 1):
            total = folded(inner, half, examples, rank, e)
            for partial in partials:
                total = total + partial[half, pl.ds(e * rank, rank), :]
            joined[pl.ds(half * rank, rank), pl.ds(e * k2, k2)] = total
    projected = mm(rows, joined[...], NN, HIGHEST)
    base = projected[:, examples * k2 :]
    for e in range(examples):
        proj = projected[:, e * k2 : (e + 1) * k2] + base
        direction = proj * lax.rsqrt(jnp.sum(proj * proj) / size + epsilon)
        dirs_out[e] = direction
        scores_out[e] = jnp.sum(direction * val_dir) / math.sqrt(size)


def chunk(slots, count, block_of, copies_of, n_copies, parts, moments, x, g, columns, top, bottom, last=None):
    tokens, width = x.shape
    k2 = columns.shape[1]
    span = width // slots.shape[0]
    quarter, rank = parts
    pieces = 2 * rank // quarter
    examples = top.shape[0] // rank
    scratch = [
        pltpu.VMEM((count, tokens, span), jnp.bfloat16),
        pltpu.VMEM((count, tokens, span), jnp.bfloat16),
        pltpu.VMEM((count, span, k2), jnp.float32),
        pltpu.VMEM((count, pieces, 2, quarter, span), jnp.bfloat16),
        pltpu.VMEM((2, (examples + 2) * rank, span), jnp.bfloat16),
        pltpu.VMEM((2, (examples + 2) * rank, 2 * k2), jnp.float32),
        pltpu.SemaphoreType.DMA((count, 3 + n_copies)),
    ]
    cost = pl.CostEstimate(
        flops=4 * tokens * span * count * rank * examples,
        bytes_accessed=6_000_000 * count,
        transcendentals=0,
    )
    common = [SMEM] + [ANY] * len(moments) + [ANY, ANY, ANY, VMEM, VMEM]
    operands = [slots, *moments, x, g, columns, top, bottom]
    params = pltpu.CompilerParams(vmem_limit_bytes=CHUNK_LIMIT)
    if last is None:
        return pl.pallas_call(
            functools.partial(chunk_kernel, block_of, copies_of, len(moments)),
            in_specs=common,
            out_specs=VMEM,
            out_shape=jax.ShapeDtypeStruct((2, (examples + 1) * rank, k2), jnp.float32),
            scratch_shapes=scratch,
            compiler_params=params,
            cost_estimate=cost,
            name="chunk",
        )(*operands)
    rows_t, val_parts, partials = last
    k1 = rows_t.shape[0]
    return pl.pallas_call(
        functools.partial(last_kernel, block_of, copies_of, len(moments), len(partials)),
        in_specs=common + [VMEM] * (3 + len(partials)),
        out_specs=[VMEM, VMEM, SMEM],
        out_shape=[
            jax.ShapeDtypeStruct((examples, k1, k2), jnp.float32),
            jax.ShapeDtypeStruct((k1, k2), jnp.float32),
            jax.ShapeDtypeStruct((examples,), jnp.float32),
        ],
        scratch_shapes=[pltpu.VMEM((2 * rank, (examples + 1) * k2), jnp.float32), *scratch],
        compiler_params=params,
        cost_estimate=cost,
        name="last_chunk",
    )(*operands, rows_t, *val_parts, *partials)


def copies_of_pieces(moments, b, target):
    group = lax.axis_index("dp")
    return [(piece.at[b], target.at[lax.bitwise_xor(group, j)]) for j, piece in enumerate(moments)]


def copies_of_blocks(moments, b, target):
    return [(moments[2 * b + k], target.at[:, k]) for k in (0, 1)]


def copies_of_gathered(moments, b, target):
    return [(moments[k].at[b], target.at[:, k]) for k in (0, 1)]


def slot_at(other, hop):
    return lax.bitwise_xor(lax.axis_index("shard"), 2 * hop + other)


def exchange(value, axis, bits):
    size = lax.axis_size(axis)
    return lax.ppermute(value, axis, [(i, i ^ bits) for i in range(size)])


def body(
    training_inputs,
    training_cotangents,
    validation_inputs,
    validation_cotangents,
    adapter_down,
    adapter_up,
    adam_first_moment,
    adam_second_moment,
    slot_block_index,
    example_lengths,
    projection_rows,
    projection_columns,
):
    groups = lax.axis_size("dp")
    shards = lax.axis_size("shard")
    rank = adapter_up.shape[0]
    quarter = 2 * rank // groups
    parts = (quarter, rank)
    stepwise = groups == 4 and shards == 8
    rows_t = projection_rows.T
    own = [m.reshape(groups, quarter, -1) for m in (adam_first_moment, adam_second_moment)]
    train = (training_inputs, training_cotangents)
    if stepwise:
        piece = cut_piece(*own)
        sibling = [exchange(m, "shard", 1) for m in own]
        far = [exchange(piece, "shard", 2 * hop) for hop in (1, 2, 3)]
        validation_inputs, _ = lax.optimization_barrier((validation_inputs, piece))
    down_t = adapter_down.T
    val_part = validation(
        validation_inputs, validation_cotangents, down_t, adapter_up, projection_columns, rows_t
    )
    lengths, val_part = lax.optimization_barrier((example_lengths[0, 0], val_part))
    top, bottom = prepare(lengths, *train, down_t, adapter_up)
    if stepwise:
        val_part, *sibling, far[0] = lax.optimization_barrier((val_part, *sibling, far[0]))
        near = [exchange(val_part, "dp", bits) for bits in (1, 2, 3)]
        *arrived, top, bottom = lax.optimization_barrier((*far, *near, top, bottom))
        far, near = jnp.stack(arrived[:3]), arrived[3:]
        four = [far] + [exchange(far, "dp", bits) for bits in (1, 2, 3)]
        total = (val_part + near[0]) + (near[1] + near[2])
        total = total + exchange(total, "shard", 2)
        total, top, bottom = lax.optimization_barrier((total, top, bottom))
        other = exchange(total, "shard", 4)
        operands = (*train, projection_columns, top, bottom)
        first = chunk(
            slot_block_index, 2, lambda b: slot_at(b, 0), copies_of_blocks, 2, parts, own + sibling, *operands
        )
        first, other, *four = lax.optimization_barrier((first, other, *four))
        total = total + other
        val_parts = [total, exchange(total, "shard", 1)]
        crossed = [exchange(part, "shard", 1) for part in four]
        second = chunk(
            slot_block_index, 3, lambda b: slot_at(0, b + 1), copies_of_pieces, 4, parts, four, *operands
        )
        partials = [first, second]
        dirs, val_dir, scores = chunk(
            slot_block_index,
            3,
            lambda b: slot_at(1, b + 1),
            copies_of_pieces,
            4,
            parts,
            crossed,
            *operands,
            last=(rows_t, val_parts, partials),
        )
    else:
        operands = (*train, projection_columns, top, bottom)
        gathered = [lax.all_gather(m, "shard", axis=0, tiled=False) for m in own]
        val_sum = lax.psum(val_part, ("dp", "shard"))
        dirs, val_dir, scores = chunk(
            slot_block_index,
            shards,
            lambda b: b,
            copies_of_gathered,
            2,
            parts,
            gathered,
            *operands,
            last=(rows_t, [val_sum, jnp.zeros_like(val_sum)], []),
        )
    return (
        dirs.reshape(1, 1, dirs.shape[0], -1),
        val_dir.reshape(-1),
        scores[None, None],
    )


def solution(mesh):
    return jax.shard_map(
        body,
        mesh=mesh,
        in_specs=(
            P(("dp", "shard"), None),
            P(("dp", "shard"), None),
            P(("dp", "shard"), None),
            P(("dp", "shard"), None),
            P(),
            P(),
            P("shard", None, None),
            P("shard", None, None),
            P(),
            P("dp", "shard", None),
            P(),
            P(),
        ),
        out_specs=(P("dp", "shard", None, None), P(), P("dp", "shard", None)),
        check_vma=False,
    )
```

```python
import functools
import math

import jax
import jax.numpy as jnp
from jax import lax
from jax.experimental import pallas as pl
from jax.experimental.pallas import tpu as pltpu
from jax.sharding import PartitionSpec as P

epsilon = 1e-06
update_scale = 0.1 / math.sqrt(0.001)
HIGHEST = lax.Precision.HIGHEST
NN = (((1,), (0,)), ((), ()))
TN = (((0,), (0,)), ((), ()))
NT = (((1,), (1,)), ((), ()))
VMEM_LIMIT = 60 * 1024 * 1024
CHUNK_LIMIT = 24 * 1024 * 1024
ANY = pl.BlockSpec(memory_space=pl.ANY)
SMEM = pl.BlockSpec(memory_space=pltpu.SMEM)
VMEM = pl.BlockSpec(memory_space=pltpu.VMEM)


def mm(a, b, dims=NN, precision=None):
    return lax.dot_general(a, b, dims, precision=precision, preferred_element_type=jnp.float32)


def two_terms(exact):
    coarse = exact.astype(jnp.bfloat16)
    fine = (exact - coarse.astype(jnp.float32)).astype(jnp.bfloat16)
    return coarse, fine


def cut_kernel(first, second, out, sems):
    group = lax.axis_index("dp")
    quarter = first.shape[1]
    copies = [
        pltpu.make_async_copy(source.at[group], out.at[pl.ds(i * quarter, quarter)], sems.at[i])
        for i, source in enumerate((first, second))
    ]
    for copy in copies:
        copy.start()
    for copy in copies:
        copy.wait()


def cut_piece(first, second):
    return pl.pallas_call(
        cut_kernel,
        in_specs=[ANY, ANY],
        out_specs=VMEM,
        out_shape=jax.ShapeDtypeStruct((2 * first.shape[1], first.shape[2]), first.dtype),
        scratch_shapes=[pltpu.SemaphoreType.DMA((2,))],
        compiler_params=pltpu.CompilerParams(vmem_limit_bytes=VMEM_LIMIT),
        name="cut_piece",
    )(first, second)


def pack_kernel(first, second, third, val, near1, near2, near3, out):
    rows = first.shape[0]
    for i, part in enumerate((first, second, third)):
        out[pl.ds(i * rows, rows), :] = part[...]
    total = (val[...] + near1[...]) + (near2[...] + near3[...])
    wide = fold(total, out.shape[1] // total.shape[1])
    coarse = wide.astype(jnp.bfloat16).astype(jnp.float32)
    terms = jnp.concatenate([coarse, wide - coarse], axis=0)
    out[pl.ds(3 * rows, terms.shape[0]), :] = terms.astype(jnp.bfloat16)


def fold(tall, times):
    rows = tall.shape[0] // times
    return jnp.concatenate([tall[i * rows : (i + 1) * rows] for i in range(times)], axis=1)


def unfold(wide, times):
    cols = wide.shape[1] // times
    return jnp.concatenate([wide[:, i * cols : (i + 1) * cols] for i in range(times)], axis=0)


def pack(far, val, near):
    rows, span = far[0].shape
    return pl.pallas_call(
        pack_kernel,
        in_specs=[VMEM] * 7,
        out_specs=VMEM,
        out_shape=jax.ShapeDtypeStruct((3 * rows + 2 * val.size // span, span), far[0].dtype),
        compiler_params=pltpu.CompilerParams(vmem_limit_bytes=CHUNK_LIMIT),
        name="pack",
    )(*far, val, *near)


def columns_loop(pairs, sems, start, step):
    steps = sems.shape[0]

    def copies(i):
        found = []
        for k, (source, target, axis) in enumerate(pairs):
            span = source.shape[axis] // steps
            at = (slice(None),) * axis + (pl.ds(pl.multiple_of(i * span, span), span),)
            found.append(pltpu.make_async_copy(source.at[at], target.at[at], sems.at[i, k]))
        return found

    for i in range(steps):
        for copy in copies(i):
            copy.start()
    span = pairs[0][0].shape[pairs[0][2]] // steps

    def one(i, total):
        for copy in copies(i):
            copy.wait()
        return step(pl.ds(pl.multiple_of(i * span, span), span), total)

    return lax.fori_loop(0, steps, one, start)


def zeros(*shape):
    return jnp.zeros(shape, jnp.float32)


def validation_kernel(xv, gv, down_t, up, columns, rows_t, proj_out, xvs, gvs, downs, ups, tables, sems):
    pairs = [(xv, xvs, 1), (gv, gvs, 1), (up, ups, 1), (down_t, downs, 1), (columns, tables, 0)]
    tokens, rank, k2 = xv.shape[0], up.shape[0], columns.shape[1]

    def step(cols, total):
        back, fwd, mixed = total
        table = jnp.concatenate(two_terms(tables[cols, :]), axis=1)
        both = jnp.concatenate([xvs[:, cols], gvs[:, cols]], axis=0)
        return (
            back + mm(gvs[:, cols], ups[:, cols], NT),
            fwd + mm(xvs[:, cols], downs[:, cols], NT),
            mixed + mm(both, table),
        )

    start = (zeros(tokens, rank), zeros(tokens, rank), zeros(2 * tokens, 2 * k2))
    back, fwd, mixed = columns_loop(pairs, sems, start, step)
    mixed = mixed[:, :k2] + mixed[:, k2:]
    inner_top = mm(back.astype(jnp.bfloat16).astype(jnp.float32), mixed[:tokens], TN, HIGHEST)
    inner_bottom = mm(fwd.astype(jnp.bfloat16).astype(jnp.float32), mixed[tokens:], TN, HIGHEST)
    inner = jnp.concatenate([inner_top, inner_bottom], axis=0)
    proj_out[...] = mm(rows_t[...], inner, NN, HIGHEST)


def prepare_kernel(lengths, x, g, down_t, up, top_out, bottom_out, xs, gs, downs, ups, sems):
    tokens, rank = x.shape[0], up.shape[0]

    def step(cols, total):
        back, fwd = total
        return back + mm(gs[:, cols], ups[:, cols], NT), fwd + mm(xs[:, cols], downs[:, cols], NT)

    pairs = [(g, gs, 1), (up, ups, 1), (x, xs, 1), (down_t, downs, 1)]
    back, fwd = columns_loop(pairs, sems, (zeros(tokens, rank), zeros(tokens, rank)), step)
    position = lax.broadcasted_iota(jnp.int32, (rank, tokens), 1)
    back_t = back.T
    fwd_t = fwd.T
    begin = jnp.int32(0)
    for e in range(lengths.shape[0]):
        finish = begin + lengths[e]
        member = (position >= begin) & (position < finish)
        top_out[pl.ds(e * rank, rank), :] = jnp.where(member, back_t, 0.0).astype(jnp.bfloat16)
        bottom_out[pl.ds(e * rank, rank), :] = jnp.where(member, fwd_t, 0.0).astype(jnp.bfloat16)
        begin = finish


STEPS = 8


def validation(xv, gv, down_t, up, columns, rows_t):
    return pl.pallas_call(
        validation_kernel,
        in_specs=[ANY] * 5 + [VMEM],
        out_specs=VMEM,
        out_shape=jax.ShapeDtypeStruct((rows_t.shape[0], columns.shape[1]), jnp.float32),
        scratch_shapes=[
            *(pltpu.VMEM(a.shape, a.dtype) for a in (xv, gv, down_t, up, columns)),
            pltpu.SemaphoreType.DMA((STEPS, 5)),
        ],
        compiler_params=pltpu.CompilerParams(vmem_limit_bytes=VMEM_LIMIT),
        cost_estimate=pl.CostEstimate(flops=10**6, bytes_accessed=10**6, transcendentals=0),
        name="validation",
    )(xv, gv, down_t, up, columns, rows_t)


def prepare(lengths, x, g, down_t, up):
    shape = jax.ShapeDtypeStruct((lengths.shape[0] * up.shape[0], x.shape[0]), jnp.bfloat16)
    return pl.pallas_call(
        prepare_kernel,
        in_specs=[SMEM] + [ANY] * 4,
        out_specs=[VMEM] * 2,
        out_shape=[shape, shape],
        scratch_shapes=[
            *(pltpu.VMEM(a.shape, a.dtype) for a in (x, g, down_t, up)),
            pltpu.SemaphoreType.DMA((STEPS, 4)),
        ],
        compiler_params=pltpu.CompilerParams(vmem_limit_bytes=VMEM_LIMIT),
        cost_estimate=pl.CostEstimate(flops=10**6, bytes_accessed=10**6, transcendentals=0),
        name="prepare",
    )(lengths, x, g, down_t, up)


def accumulate(block_of, copies_of, moments, slots, x, g, columns, top, bottom, xs, gs, cs, ms, update, inner, sems):
    count, _, span = xs.shape
    quarter = ms.shape[2] // 2
    rank = ms.shape[1] * quarter // 2
    examples = top.shape[0] // rank
    half_parts = ms.shape[1] // 2
    cut = min(span, 256)

    def copies(b, cols, moment_copies):
        pairs = [(x.at[:, cols], xs.at[b]), (g.at[:, cols], gs.at[b]), (columns.at[cols, :], cs.at[b])]
        pairs += moment_copies
        return [pltpu.make_async_copy(p[0], p[1], sems.at[b, k]) for k, p in enumerate(pairs)]

    for b in range(count):
        cols = pl.ds(pl.multiple_of(slots[block_of(b)] * span, span), span)
        for copy in copies(b, cols, copies_of(moments, b, ms.at[b])):
            copy.start()
    inner[...] = jnp.zeros_like(inner)

    @pl.loop(0, count)
    def _(b):
        for copy in copies(b, pl.ds(0, span), copies_of(moments, 0, ms.at[b])):
            copy.wait()

        @pl.loop(0, span // cut)
        def _(c):
            cols = pl.ds(pl.multiple_of(c * cut, cut), cut)
            grads = [mm(mask[...], source[b, :, cols]) for source, mask in ((xs, top), (gs, bottom))]
            for half, grad in enumerate(grads):
                parts = slice(half * half_parts, (half + 1) * half_parts)
                low, high = pl.ds(0, quarter), pl.ds(quarter, quarter)
                first = 9.0 * ms[b, parts, low, cols].astype(jnp.float32).reshape(rank, cut)
                second = 999.0 * ms[b, parts, high, cols].astype(jnp.float32).reshape(rank, cut)
                shared = first * lax.rsqrt(second)
                coarse, fine = two_terms(shared)
                update[half, pl.ds(examples * rank, rank), cols] = coarse
                update[half, pl.ds((examples + 1) * rank, rank), cols] = fine
                for e in range(examples):
                    piece = grad[e * rank : (e + 1) * rank]
                    change = (first + piece) * lax.rsqrt(second + piece * piece) - shared
                    update[half, pl.ds(e * rank, rank), cols] = change.astype(jnp.bfloat16)

        table = jnp.concatenate(two_terms(cs[b]), axis=1)
        for half in (0, 1):
            inner[half] += mm(update[half], table)


def folded(inner, half, examples, rank, e):
    k2 = inner.shape[2] // 2
    part = pl.ds(e * rank, rank)
    total = inner[half, part, :k2] + inner[half, part, k2:]
    if e == examples:
        part = pl.ds((examples + 1) * rank, rank)
        total = total + inner[half, part, :k2] + inner[half, part, k2:]
    return total


def chunk_kernel(block_of, copies_of, n_moments, slots, *refs):
    moments, refs = refs[:n_moments], refs[n_moments:]
    x, g, columns, top, bottom, out, xs, gs, cs, ms, update, inner, sems = refs
    accumulate(
        block_of, copies_of, moments, slots, x, g, columns, top, bottom, xs, gs, cs, ms, update, inner, sems
    )
    rank = ms.shape[1] * ms.shape[2] // 4
    examples = top.shape[0] // rank
    for half in (0, 1):
        for e in range(examples + 1):
            out[half, pl.ds(e * rank, rank), :] = folded(inner, half, examples, rank, e)


def last_kernel(block_of, copies_of, n_moments, n_val, n_partial, slots, *refs):
    moments, refs = refs[:n_moments], refs[n_moments:]
    x, g, columns, top, bottom, rows_t = refs[:6]
    val_parts, refs = refs[6 : 6 + n_val], refs[6 + n_val :]
    partials, refs = refs[:n_partial], refs[n_partial:]
    dirs_out, val_out, scores_out, joined, vals, val_sems, xs, gs, cs, ms, update, inner, sems = refs
    val_rows = vals.shape[1]
    val_copies = []
    if n_val > 1:
        val_copies = [
            pltpu.make_async_copy(part.at[pl.ds(part.shape[0] - val_rows, val_rows)], vals.at[i], val_sems.at[i])
            for i, part in enumerate(val_parts)
        ]
    for copy in val_copies:
        copy.start()
    accumulate(
        block_of, copies_of, moments, slots, x, g, columns, top, bottom, xs, gs, cs, ms, update, inner, sems
    )
    rank = ms.shape[1] * ms.shape[2] // 4
    examples = top.shape[0] // rank
    k1, k2 = rows_t.shape[0], columns.shape[1]
    size = k1 * k2
    for copy in val_copies:
        copy.wait()
    if n_val > 1:
        terms = [vals[i].astype(jnp.float32) for i in range(n_val)]
        terms = [term[: val_rows // 2] + term[val_rows // 2 :] for term in terms]
        half = [(t[0] + t[1]) + (t[2] + t[3]) for t in (terms[:4], terms[4:])]
        val = unfold(half[0] + half[1], vals.shape[2] // k2)
    else:
        val = val_parts[0][...]
    val_dir = val * lax.rsqrt(jnp.sum(val * val) / size + epsilon)
    val_out[...] = val_dir
    rows = rows_t[...] * update_scale
    for e in range(examples + 1):
        for half in (0, 1):
            total = folded(inner, half, examples, rank, e)
            for partial in partials:
                total = total + partial[half, pl.ds(e * rank, rank), :]
            joined[pl.ds(half * rank, rank), pl.ds(e * k2, k2)] = total
    projected = mm(rows, joined[...], NN, HIGHEST)
    base = projected[:, examples * k2 :]
    for e in range(examples):
        proj = projected[:, e * k2 : (e + 1) * k2] + base
        direction = proj * lax.rsqrt(jnp.sum(proj * proj) / size + epsilon)
        dirs_out[e] = direction
        scores_out[e] = jnp.sum(direction * val_dir) / math.sqrt(size)


def chunk(slots, count, block_of, copies_of, n_copies, parts, moments, x, g, columns, top, bottom, last=None):
    tokens, width = x.shape
    k2 = columns.shape[1]
    span = width // slots.shape[0]
    quarter, rank = parts
    pieces = 2 * rank // quarter
    examples = top.shape[0] // rank
    scratch = [
        pltpu.VMEM((count, tokens, span), jnp.bfloat16),
        pltpu.VMEM((count, tokens, span), jnp.bfloat16),
        pltpu.VMEM((count, span, k2), jnp.float32),
        pltpu.VMEM((count, pieces, 2 * quarter, span), jnp.bfloat16),
        pltpu.VMEM((2, (examples + 2) * rank, span), jnp.bfloat16),
        pltpu.VMEM((2, (examples + 2) * rank, 2 * k2), jnp.float32),
        pltpu.SemaphoreType.DMA((count, 3 + n_copies)),
    ]
    cost = pl.CostEstimate(
        flops=10**6,
        bytes_accessed=10**6,
        transcendentals=0,
    )
    common = [SMEM] + [ANY] * len(moments) + [ANY, ANY, ANY, VMEM, VMEM]
    operands = [slots, *moments, x, g, columns, top, bottom]
    params = pltpu.CompilerParams(vmem_limit_bytes=CHUNK_LIMIT)
    if last is None:
        return pl.pallas_call(
            functools.partial(chunk_kernel, block_of, copies_of, len(moments)),
            in_specs=common,
            out_specs=VMEM,
            out_shape=jax.ShapeDtypeStruct((2, (examples + 1) * rank, k2), jnp.float32),
            scratch_shapes=scratch,
            compiler_params=params,
            cost_estimate=cost,
            name="chunk",
        )(*operands)
    rows_t, val_parts, partials = last
    k1 = rows_t.shape[0]
    packed = len(val_parts) > 1
    val_shape = (len(val_parts), 2 * k1 * k2 // span if packed else 8, span)
    return pl.pallas_call(
        functools.partial(last_kernel, block_of, copies_of, len(moments), len(val_parts), len(partials)),
        in_specs=common + [VMEM] + [ANY if packed else VMEM] * len(val_parts) + [VMEM] * len(partials),
        out_specs=[VMEM, VMEM, SMEM],
        out_shape=[
            jax.ShapeDtypeStruct((examples, k1, k2), jnp.float32),
            jax.ShapeDtypeStruct((k1, k2), jnp.float32),
            jax.ShapeDtypeStruct((examples,), jnp.float32),
        ],
        scratch_shapes=[
            pltpu.VMEM((2 * rank, (examples + 1) * k2), jnp.float32),
            pltpu.VMEM(val_shape, jnp.bfloat16),
            pltpu.SemaphoreType.DMA((len(val_parts),)),
            *scratch,
        ],
        compiler_params=params,
        cost_estimate=cost,
        name="last_chunk",
    )(*operands, rows_t, *val_parts, *partials)


def copies_of_pieces(moments, b, target):
    group = lax.axis_index("dp")
    rows = target.shape[1]
    return [
        (piece.at[pl.ds(b * rows, rows)], target.at[lax.bitwise_xor(group, j)]) for j, piece in enumerate(moments)
    ]


def both_moments(first, second, target):
    quarter = target.shape[1] // 2
    return [(first, target.at[:, pl.ds(0, quarter)]), (second, target.at[:, pl.ds(quarter, quarter)])]


def copies_of_blocks(moments, b, target):
    return both_moments(moments[2 * b], moments[2 * b + 1], target)


def copies_of_gathered(moments, b, target):
    return both_moments(moments[0].at[b], moments[1].at[b], target)


def slot_at(other, hop):
    return lax.bitwise_xor(lax.axis_index("shard"), 2 * hop + other)


def exchange(value, axis, bits):
    size = lax.axis_size(axis)
    return lax.ppermute(value, axis, [(i, i ^ bits) for i in range(size)])


def body(
    training_inputs,
    training_cotangents,
    validation_inputs,
    validation_cotangents,
    adapter_down,
    adapter_up,
    adam_first_moment,
    adam_second_moment,
    slot_block_index,
    example_lengths,
    projection_rows,
    projection_columns,
):
    groups = lax.axis_size("dp")
    shards = lax.axis_size("shard")
    rank = adapter_up.shape[0]
    quarter = 2 * rank // groups
    parts = (quarter, rank)
    stepwise = groups == 4 and shards == 8
    rows_t = projection_rows.T
    own = [m.reshape(groups, quarter, -1) for m in (adam_first_moment, adam_second_moment)]
    train = (training_inputs, training_cotangents)
    if stepwise:
        piece = cut_piece(*own)
        sibling = [exchange(m, "shard", 1) for m in own]
        far = [exchange(piece, "shard", 2 * hop) for hop in (1, 2, 3)]
        validation_inputs, _ = lax.optimization_barrier((validation_inputs, piece))
    down_t = adapter_down.T
    val_part = validation(
        validation_inputs, validation_cotangents, down_t, adapter_up, projection_columns, rows_t
    )
    lengths, val_part = lax.optimization_barrier((example_lengths[0, 0], val_part))
    top, bottom = prepare(lengths, *train, down_t, adapter_up)
    if stepwise:
        val_part, *sibling, far[0] = lax.optimization_barrier((val_part, *sibling, far[0]))
        near = [exchange(val_part, "shard", 2 * hop) for hop in (1, 2, 3)]
        *arrived, top, bottom = lax.optimization_barrier((*far, *near, top, bottom))
        far = pack(arrived[:3], val_part, arrived[3:])
        four = [far] + [exchange(far, "dp", bits) for bits in (1, 2, 3)]
        operands = (*train, projection_columns, top, bottom)
        first = chunk(
            slot_block_index, 2, lambda b: slot_at(b, 0), copies_of_blocks, 2, parts, own + sibling, *operands
        )
        first, *four = lax.optimization_barrier((first, *four))
        crossed = [exchange(part, "shard", 1) for part in four]
        second = chunk(
            slot_block_index, 3, lambda b: slot_at(0, b + 1), copies_of_pieces, 4, parts, four, *operands
        )
        partials = [first, second]
        dirs, val_dir, scores = chunk(
            slot_block_index,
            3,
            lambda b: slot_at(1, b + 1),
            copies_of_pieces,
            4,
            parts,
            crossed,
            *operands,
            last=(rows_t, four + crossed, partials),
        )
    else:
        operands = (*train, projection_columns, top, bottom)
        gathered = [lax.all_gather(m, "shard", axis=0, tiled=False) for m in own]
        val_sum = lax.psum(val_part, ("dp", "shard"))
        dirs, val_dir, scores = chunk(
            slot_block_index,
            shards,
            lambda b: b,
            copies_of_gathered,
            2,
            parts,
            gathered,
            *operands,
            last=(rows_t, [val_sum], []),
        )
    return (
        dirs.reshape(1, 1, dirs.shape[0], -1),
        val_dir.reshape(-1),
        scores[None, None],
    )


def solution(mesh):
    return jax.shard_map(
        body,
        mesh=mesh,
        in_specs=(
            P(("dp", "shard"), None),
            P(("dp", "shard"), None),
            P(("dp", "shard"), None),
            P(("dp", "shard"), None),
            P(),
            P(),
            P("shard", None, None),
            P("shard", None, None),
            P(),
            P("dp", "shard", None),
            P(),
            P(),
        ),
        out_specs=(P("dp", "shard", None, None), P(), P("dp", "shard", None)),
        check_vma=False,
    )
```

```python
import functools
import math

import jax
import jax.numpy as jnp
from jax import lax
from jax.experimental import pallas as pl
from jax.experimental.pallas import tpu as pltpu
from jax.sharding import PartitionSpec as P

epsilon = 1e-06
update_scale = 0.1 / math.sqrt(0.001)
HIGHEST = lax.Precision.HIGHEST
NN = (((1,), (0,)), ((), ()))
TN = (((0,), (0,)), ((), ()))
NT = (((1,), (1,)), ((), ()))
VMEM_LIMIT = 60 * 1024 * 1024
CHUNK_LIMIT = 24 * 1024 * 1024
ANY = pl.BlockSpec(memory_space=pl.ANY)
SMEM = pl.BlockSpec(memory_space=pltpu.SMEM)
VMEM = pl.BlockSpec(memory_space=pltpu.VMEM)


def mm(a, b, dims=NN, precision=None):
    return lax.dot_general(a, b, dims, precision=precision, preferred_element_type=jnp.float32)


def two_terms(exact):
    coarse = exact.astype(jnp.bfloat16)
    fine = (exact - coarse.astype(jnp.float32)).astype(jnp.bfloat16)
    return coarse, fine


def cut_kernel(first, second, out, sems):
    group = lax.axis_index("dp")
    quarter = first.shape[1]
    copies = [
        pltpu.make_async_copy(source.at[group], out.at[pl.ds(i * quarter, quarter)], sems.at[i])
        for i, source in enumerate((first, second))
    ]
    for copy in copies:
        copy.start()
    for copy in copies:
        copy.wait()


def cut_piece(first, second):
    return pl.pallas_call(
        cut_kernel,
        in_specs=[ANY, ANY],
        out_specs=VMEM,
        out_shape=jax.ShapeDtypeStruct((2 * first.shape[1], first.shape[2]), first.dtype),
        scratch_shapes=[pltpu.SemaphoreType.DMA((2,))],
        compiler_params=pltpu.CompilerParams(vmem_limit_bytes=VMEM_LIMIT),
        name="cut_piece",
    )(first, second)


def fold(tall, times):
    rows = tall.shape[0] // times
    return jnp.concatenate([tall[i * rows : (i + 1) * rows] for i in range(times)], axis=1)


def unfold(wide, times):
    cols = wide.shape[1] // times
    return jnp.concatenate([wide[:, i * cols : (i + 1) * cols] for i in range(times)], axis=0)


def on_vmem(kernel, shape, dtype, name, *operands):
    return pl.pallas_call(
        kernel,
        in_specs=[VMEM] * len(operands),
        out_specs=VMEM,
        out_shape=jax.ShapeDtypeStruct(shape, dtype),
        compiler_params=pltpu.CompilerParams(vmem_limit_bytes=CHUNK_LIMIT),
        name=name,
    )(*operands)


def pack_kernel(piece, val, out):
    rows = piece.shape[0]
    out[pl.ds(0, rows), :] = piece[...]
    wide = fold(val[...], out.shape[1] // val.shape[1])
    coarse = wide.astype(jnp.bfloat16).astype(jnp.float32)
    terms = jnp.concatenate([coarse, wide - coarse], axis=0)
    out[pl.ds(rows, terms.shape[0]), :] = terms.astype(jnp.bfloat16)


def pack(piece, val):
    rows, span = piece.shape
    return on_vmem(pack_kernel, (rows + 2 * val.size // span, span), piece.dtype, "pack", piece, val)


def join_kernel(first, second, out):
    rows = first.shape[0]
    out[pl.ds(0, rows), :] = first[...]
    out[pl.ds(rows, rows), :] = second[...]


def join(first, second):
    rows, span = first.shape
    return on_vmem(join_kernel, (2 * rows, span), first.dtype, "join", first, second)


def order_kernel(first, second, third, fourth, out):
    group = lax.axis_index("dp")
    for j, part in enumerate((first, second, third, fourth)):
        out[lax.bitwise_xor(group, j)] = part[...]


def order(four):
    return on_vmem(order_kernel, (4,) + four[0].shape, four[0].dtype, "order", *four)


def plane_kernel(rows, own, crossed, out):
    total = None
    for part in (own, crossed):
        terms = [part[q, rows:, :].astype(jnp.float32) for q in range(4)]
        terms = [term[: term.shape[0] // 2] + term[term.shape[0] // 2 :] for term in terms]
        found = (terms[0] + terms[1]) + (terms[2] + terms[3])
        total = found if total is None else total + found
    out[...] = unfold(total, total.shape[1] // out.shape[1])


def plane_sum(rows, shape, own, crossed):
    return on_vmem(functools.partial(plane_kernel, rows), shape, jnp.float32, "plane_sum", own, crossed)


def zeros(*shape):
    return jnp.zeros(shape, jnp.float32)


def split_copies(source, target, axis, count, sems, first):
    span = source.shape[axis] // count
    found = []
    for i in range(count):
        at = (slice(None),) * axis + (pl.ds(i * span, span),)
        found.append(pltpu.make_async_copy(source.at[at], target.at[at], sems.at[first + i]))
    return found


PARTS = 4
HALVES = 2


def validation_kernel(xv, gv, down_t, up, columns, rows_t, proj_out, xvs, gvs, downs, ups, tables, sems):
    tokens, width = xv.shape
    k2 = columns.shape[1]
    pairs = [(gv, gvs), (up, ups), (xv, xvs), (down_t, downs)]
    whole = [pltpu.make_async_copy(p[0], p[1], sems.at[i]) for i, p in enumerate(pairs)]
    parts = split_copies(columns, tables, 0, PARTS, sems, len(pairs))
    for copy in whole + parts:
        copy.start()
    whole[0].wait()
    whole[1].wait()
    back = mm(gvs[...], ups[...], NT)
    whole[2].wait()
    whole[3].wait()
    fwd = mm(xvs[...], downs[...], NT)
    mixed = zeros(2 * tokens, 2 * k2)
    span = width // PARTS
    for i in range(PARTS):
        parts[i].wait()
        cols = pl.ds(i * span, span)
        table = jnp.concatenate(two_terms(tables[cols, :]), axis=1)
        mixed = mixed + mm(jnp.concatenate([xvs[:, cols], gvs[:, cols]], axis=0), table)
    mixed = mixed[:, :k2] + mixed[:, k2:]
    inner_top = mm(back.astype(jnp.bfloat16).astype(jnp.float32), mixed[:tokens], TN, HIGHEST)
    inner_bottom = mm(fwd.astype(jnp.bfloat16).astype(jnp.float32), mixed[tokens:], TN, HIGHEST)
    inner = jnp.concatenate([inner_top, inner_bottom], axis=0)
    proj_out[...] = mm(rows_t[...], inner, NN, HIGHEST)


def prepare_kernel(lengths, x, g, down_t, up, top_out, bottom_out, xs, gs, downs, ups, sems):
    tokens, width = x.shape
    examples, rank = lengths.shape[0], up.shape[0]
    copies = []
    for i, (source, target) in enumerate(((up, ups), (g, gs), (down_t, downs), (x, xs))):
        copies.append(split_copies(source, target, 1, HALVES, sems, i * HALVES))
    for i in range(HALVES):
        for pair in copies[:2]:
            pair[i].start()
    for i in range(HALVES):
        for pair in copies[2:]:
            pair[i].start()
    span = width // HALVES
    position = lax.broadcasted_iota(jnp.int32, (rank, tokens), 1)
    for first, (left, right, out) in enumerate(((gs, ups, top_out), (xs, downs, bottom_out))):
        total = zeros(tokens, rank)
        for i in range(HALVES):
            copies[2 * first][i].wait()
            copies[2 * first + 1][i].wait()
            cols = pl.ds(i * span, span)
            total = total + mm(left[:, cols], right[:, cols], NT)
        turned = total.T
        begin = jnp.int32(0)
        for e in range(examples):
            finish = begin + lengths[e]
            member = (position >= begin) & (position < finish)
            out[pl.ds(e * rank, rank), :] = jnp.where(member, turned, 0.0).astype(jnp.bfloat16)
            begin = finish


def validation(xv, gv, down_t, up, columns, rows_t):
    return pl.pallas_call(
        validation_kernel,
        in_specs=[ANY] * 5 + [VMEM],
        out_specs=VMEM,
        out_shape=jax.ShapeDtypeStruct((rows_t.shape[0], columns.shape[1]), jnp.float32),
        scratch_shapes=[
            *(pltpu.VMEM(a.shape, a.dtype) for a in (xv, gv, down_t, up, columns)),
            pltpu.SemaphoreType.DMA((4 + PARTS,)),
        ],
        compiler_params=pltpu.CompilerParams(vmem_limit_bytes=VMEM_LIMIT),
        cost_estimate=pl.CostEstimate(flops=10**6, bytes_accessed=10**6, transcendentals=0),
        name="validation",
    )(xv, gv, down_t, up, columns, rows_t)


def prepare(lengths, x, g, down_t, up):
    shape = jax.ShapeDtypeStruct((lengths.shape[0] * up.shape[0], x.shape[0]), jnp.bfloat16)
    return pl.pallas_call(
        prepare_kernel,
        in_specs=[SMEM] + [ANY] * 4,
        out_specs=[VMEM] * 2,
        out_shape=[shape, shape],
        scratch_shapes=[
            *(pltpu.VMEM(a.shape, a.dtype) for a in (x, g, down_t, up)),
            pltpu.SemaphoreType.DMA((4 * HALVES,)),
        ],
        compiler_params=pltpu.CompilerParams(vmem_limit_bytes=VMEM_LIMIT),
        cost_estimate=pl.CostEstimate(flops=10**6, bytes_accessed=10**6, transcendentals=0),
        name="prepare",
    )(lengths, x, g, down_t, up)


def accumulate(blocks, moments, slots, x, g, columns, top, bottom, update, inner):
    _, rows2, span = update.shape
    rank = (rows2 - top.shape[0]) // 2
    examples = top.shape[0] // rank
    cut = min(span, 256)
    starts = [pl.multiple_of(slots[slot_of()] * span, span) for slot_of, _ in blocks]
    tiles = [(b, half, c) for b in range(len(blocks)) for half in (0, 1) for c in range(0, span, cut)]
    sources, masks = (x, g), (top, bottom)

    def gradient(tile):
        b, half, c = tile
        cols = pl.ds(pl.multiple_of(starts[b] + c, cut), cut)
        return mm(masks[half][...], sources[half][:, cols])

    def moment(b, k, half, cols):
        ref, low, quarter = blocks[b][1](moments, k)
        parts = ref.shape[0] // 2
        found = ref[half * parts : (half + 1) * parts, low : low + quarter, cols]
        return found.astype(jnp.float32).reshape(rank, cut)

    def elementwise(tile, grad):
        b, half, c = tile
        cols = pl.ds(c, cut)
        first = 9.0 * moment(b, 0, half, cols)
        second = 999.0 * moment(b, 1, half, cols)
        shared = first * lax.rsqrt(second)
        coarse, fine = two_terms(shared)
        update[half, pl.ds(examples * rank, rank), cols] = coarse
        update[half, pl.ds((examples + 1) * rank, rank), cols] = fine
        for e in range(examples):
            piece = grad[e * rank : (e + 1) * rank]
            change = (first + piece) * lax.rsqrt(second + piece * piece) - shared
            update[half, pl.ds(e * rank, rank), cols] = change.astype(jnp.bfloat16)

    grad = gradient(tiles[0])
    for i, tile in enumerate(tiles):
        following = gradient(tiles[i + 1]) if i + 1 < len(tiles) else None
        elementwise(tile, grad)
        grad = following
        b, half, c = tile
        if c + cut == span:
            if half == 0:
                table = jnp.concatenate(two_terms(columns[pl.ds(starts[b], span), :]), axis=1)
            product = mm(update[half], table)
            inner[half] = product if b == 0 else inner[half] + product


def folded(inner, half, examples, rank, e):
    k2 = inner.shape[2] // 2
    part = pl.ds(e * rank, rank)
    total = inner[half, part, :k2] + inner[half, part, k2:]
    if e == examples:
        part = pl.ds((examples + 1) * rank, rank)
        total = total + inner[half, part, :k2] + inner[half, part, k2:]
    return total


def chunk_kernel(blocks, n_moments, slots, *refs):
    moments, refs = refs[:n_moments], refs[n_moments:]
    x, g, columns, top, bottom, out, update, inner = refs
    accumulate(blocks, moments, slots, x, g, columns, top, bottom, update, inner)
    rank = (update.shape[1] - top.shape[0]) // 2
    examples = top.shape[0] // rank
    for half in (0, 1):
        for e in range(examples + 1):
            out[half, pl.ds(e * rank, rank), :] = folded(inner, half, examples, rank, e)


def last_kernel(blocks, n_moments, n_val, n_partial, slots, *refs):
    moments, refs = refs[:n_moments], refs[n_moments:]
    x, g, columns, top, bottom, rows_t = refs[:6]
    val_parts, refs = refs[6 : 6 + n_val], refs[6 + n_val :]
    partials, refs = refs[:n_partial], refs[n_partial:]
    dirs_out, val_out, scores_out, joined, update, inner = refs
    accumulate(blocks, moments, slots, x, g, columns, top, bottom, update, inner)
    rank = (update.shape[1] - top.shape[0]) // 2
    examples = top.shape[0] // rank
    k1, k2 = rows_t.shape[0], columns.shape[1]
    size = k1 * k2
    val = val_parts[0][...]
    for part in val_parts[1:]:
        val = val + part[...]
    val_dir = val * lax.rsqrt(jnp.sum(val * val) / size + epsilon)
    val_out[...] = val_dir
    rows = rows_t[...] * update_scale
    for e in range(examples + 1):
        for half in (0, 1):
            total = folded(inner, half, examples, rank, e)
            for partial in partials:
                total = total + partial[half, pl.ds(e * rank, rank), :]
            joined[pl.ds(half * rank, rank), pl.ds(e * k2, k2)] = total
    projected = mm(rows, joined[...], NN, HIGHEST)
    base = projected[:, examples * k2 :]
    for e in range(examples):
        proj = projected[:, e * k2 : (e + 1) * k2] + base
        direction = proj * lax.rsqrt(jnp.sum(proj * proj) / size + epsilon)
        dirs_out[e] = direction
        scores_out[e] = jnp.sum(direction * val_dir) / math.sqrt(size)


def chunk(slots, blocks, moments, x, g, columns, top, bottom, rank, last=None):
    tokens, width = x.shape
    k2 = columns.shape[1]
    span = width // slots.shape[0]
    examples = top.shape[0] // rank
    scratch = [
        pltpu.VMEM((2, (examples + 2) * rank, span), jnp.bfloat16),
        pltpu.VMEM((2, (examples + 2) * rank, 2 * k2), jnp.float32),
    ]
    common = [SMEM] + [VMEM] * (len(moments) + 5)
    operands = [slots, *moments, x, g, columns, top, bottom]
    options = dict(
        compiler_params=pltpu.CompilerParams(vmem_limit_bytes=CHUNK_LIMIT),
        cost_estimate=pl.CostEstimate(flops=10**6, bytes_accessed=10**6, transcendentals=0),
    )
    if last is None:
        return pl.pallas_call(
            functools.partial(chunk_kernel, blocks, len(moments)),
            in_specs=common,
            out_specs=VMEM,
            out_shape=jax.ShapeDtypeStruct((2, (examples + 1) * rank, k2), jnp.float32),
            scratch_shapes=scratch,
            name="chunk",
            **options,
        )(*operands)
    rows_t, val_parts, partials = last
    k1 = rows_t.shape[0]
    return pl.pallas_call(
        functools.partial(last_kernel, blocks, len(moments), len(val_parts), len(partials)),
        in_specs=common + [VMEM] * (1 + len(val_parts) + len(partials)),
        out_specs=[VMEM, VMEM, SMEM],
        out_shape=[
            jax.ShapeDtypeStruct((examples, k1, k2), jnp.float32),
            jax.ShapeDtypeStruct((k1, k2), jnp.float32),
            jax.ShapeDtypeStruct((examples,), jnp.float32),
        ],
        scratch_shapes=[pltpu.VMEM((2 * rank, (examples + 1) * k2), jnp.float32), *scratch],
        name="last_chunk",
        **options,
    )(*operands, rows_t, *val_parts, *partials)


def slot_at(other, hop):
    return lambda: lax.bitwise_xor(lax.axis_index("shard"), 2 * hop + other)


def ordered_block(quarter, other, hop, which, place):
    return slot_at(other, hop), lambda moments, k: (moments[which], (2 * place + k) * quarter, quarter)


def paired_block(quarter, other, which):
    return slot_at(other, 0), lambda moments, k: (moments[2 * which + k], 0, quarter)


def gathered_block(quarter, b):
    return lambda: b, lambda moments, k: (moments[k].at[b], 0, quarter)


def exchange(value, axis, bits):
    size = lax.axis_size(axis)
    return lax.ppermute(value, axis, [(i, i ^ bits) for i in range(size)])


def body(
    training_inputs,
    training_cotangents,
    validation_inputs,
    validation_cotangents,
    adapter_down,
    adapter_up,
    adam_first_moment,
    adam_second_moment,
    slot_block_index,
    example_lengths,
    projection_rows,
    projection_columns,
):
    groups = lax.axis_size("dp")
    shards = lax.axis_size("shard")
    rank = adapter_up.shape[0]
    quarter = 2 * rank // groups
    stepwise = groups == 4 and shards == 8
    rows_t = projection_rows.T
    own = [m.reshape(groups, quarter, -1) for m in (adam_first_moment, adam_second_moment)]
    train = (training_inputs, training_cotangents)
    if stepwise:
        piece = cut_piece(*own)
        sibling = [exchange(m, "shard", 1) for m in own]
        far = [exchange(piece, "shard", 2 * hop) for hop in (1, 2, 3)]
        validation_inputs, _ = lax.optimization_barrier((validation_inputs, piece))
    down_t = adapter_down.T
    val_part = validation(
        validation_inputs, validation_cotangents, down_t, adapter_up, projection_columns, rows_t
    )
    lengths, val_part = lax.optimization_barrier((example_lengths[0, 0], val_part))
    top, bottom = prepare(lengths, *train, down_t, adapter_up)
    if stepwise:
        val_part, *sibling, far[0], far[1] = lax.optimization_barrier((val_part, *sibling, far[0], far[1]))
        packed = pack(far[0], val_part)
        near = [packed] + [exchange(packed, "dp", bits) for bits in (1, 2, 3)]
        *arrived, top, bottom = lax.optimization_barrier((*far[1:], *near, top, bottom))
        rest = join(*arrived[:2])
        four = [rest] + [exchange(rest, "dp", bits) for bits in (1, 2, 3)]
        one = order(arrived[2:])
        one, top, bottom = lax.optimization_barrier((one, top, bottom))
        one_crossed = exchange(one, "shard", 1)
        operands = (*train, projection_columns, top, bottom, rank)
        slots = slot_block_index
        partials = [chunk(slots, [paired_block(quarter, i, i) for i in (0, 1)], own + sibling, *operands)]
        partials[0], one_crossed = lax.optimization_barrier((partials[0], one_crossed))
        total = plane_sum(2 * quarter, val_part.shape, one, one_crossed)
        total, one_crossed = lax.optimization_barrier((total, one_crossed))
        other = exchange(total, "shard", 2)
        partials.append(
            chunk(slots, [ordered_block(quarter, i, 1, i, 0) for i in (0, 1)], [one, one_crossed], *operands)
        )
        partials[1], other, *four = lax.optimization_barrier((partials[1], other, *four))
        total = total + other
        both = order(four)
        total, both = lax.optimization_barrier((total, both))
        val_parts = [total, exchange(total, "shard", 4)]
        both_crossed = exchange(both, "shard", 1)
        partials.append(chunk(slots, [ordered_block(quarter, 0, 2 + i, 0, i) for i in (0, 1)], [both], *operands))
        dirs, val_dir, scores = chunk(
            slots,
            [ordered_block(quarter, 1, 2 + i, 0, i) for i in (0, 1)],
            [both_crossed],
            *operands,
            last=(rows_t, val_parts, partials),
        )
    else:
        operands = (*train, projection_columns, top, bottom, rank)
        gathered = [lax.all_gather(m, "shard", axis=0, tiled=False) for m in own]
        val_sum = lax.psum(val_part, ("dp", "shard"))
        dirs, val_dir, scores = chunk(
            slot_block_index,
            [gathered_block(quarter, b) for b in range(shards)],
            gathered,
            *operands,
            last=(rows_t, [val_sum], []),
        )
    return (
        dirs.reshape(1, 1, dirs.shape[0], -1),
        val_dir.reshape(-1),
        scores[None, None],
    )


def solution(mesh):
    return jax.shard_map(
        body,
        mesh=mesh,
        in_specs=(
            P(("dp", "shard"), None),
            P(("dp", "shard"), None),
            P(("dp", "shard"), None),
            P(("dp", "shard"), None),
            P(),
            P(),
            P("shard", None, None),
            P("shard", None, None),
            P(),
            P("dp", "shard", None),
            P(),
            P(),
        ),
        out_specs=(P("dp", "shard", None, None), P(), P("dp", "shard", None)),
        check_vma=False,
    )
```

```python
import functools
import math

import jax
import jax.numpy as jnp
from jax import lax
from jax.experimental import pallas as pl
from jax.experimental.pallas import tpu as pltpu
from jax.sharding import PartitionSpec as P

epsilon = 1e-06
update_scale = 0.1 / math.sqrt(0.001)
HIGHEST = lax.Precision.HIGHEST
NN = (((1,), (0,)), ((), ()))
TN = (((0,), (0,)), ((), ()))
NT = (((1,), (1,)), ((), ()))
VMEM_LIMIT = 60 * 1024 * 1024
CHUNK_LIMIT = 24 * 1024 * 1024
ANY = pl.BlockSpec(memory_space=pl.ANY)
SMEM = pl.BlockSpec(memory_space=pltpu.SMEM)
VMEM = pl.BlockSpec(memory_space=pltpu.VMEM)


def mm(a, b, dims=NN, precision=None):
    return lax.dot_general(a, b, dims, precision=precision, preferred_element_type=jnp.float32)


def two_terms(exact):
    coarse = exact.astype(jnp.bfloat16)
    fine = (exact - coarse.astype(jnp.float32)).astype(jnp.bfloat16)
    return coarse, fine


def cut_kernel(first, second, out, sems):
    group = lax.axis_index("dp")
    quarter = first.shape[1]
    copies = [
        pltpu.make_async_copy(source.at[group], out.at[pl.ds(i * quarter, quarter)], sems.at[i])
        for i, source in enumerate((first, second))
    ]
    for copy in copies:
        copy.start()
    for copy in copies:
        copy.wait()


def cut_piece(first, second):
    return pl.pallas_call(
        cut_kernel,
        in_specs=[ANY, ANY],
        out_specs=VMEM,
        out_shape=jax.ShapeDtypeStruct((2 * first.shape[1], first.shape[2]), first.dtype),
        scratch_shapes=[pltpu.SemaphoreType.DMA((2,))],
        compiler_params=pltpu.CompilerParams(vmem_limit_bytes=VMEM_LIMIT),
        name="cut_piece",
    )(first, second)


def fold(tall, times):
    rows = tall.shape[0] // times
    return jnp.concatenate([tall[i * rows : (i + 1) * rows] for i in range(times)], axis=1)


def unfold(wide, times):
    cols = wide.shape[1] // times
    return jnp.concatenate([wide[:, i * cols : (i + 1) * cols] for i in range(times)], axis=0)


def on_vmem(kernel, shape, dtype, name, *operands):
    return pl.pallas_call(
        kernel,
        in_specs=[VMEM] * len(operands),
        out_specs=VMEM,
        out_shape=jax.ShapeDtypeStruct(shape, dtype),
        compiler_params=pltpu.CompilerParams(vmem_limit_bytes=CHUNK_LIMIT),
        name=name,
    )(*operands)


def pack_kernel(piece, val, out):
    rows = piece.shape[0]
    out[pl.ds(0, rows), :] = piece[...]
    wide = fold(val[...], out.shape[1] // val.shape[1])
    coarse = wide.astype(jnp.bfloat16).astype(jnp.float32)
    terms = jnp.concatenate([coarse, wide - coarse], axis=0)
    out[pl.ds(rows, terms.shape[0]), :] = terms.astype(jnp.bfloat16)


def pack(piece, val):
    rows, span = piece.shape
    return on_vmem(pack_kernel, (rows + 2 * val.size // span, span), piece.dtype, "pack", piece, val)


def join_kernel(first, second, out):
    rows = first.shape[0]
    out[pl.ds(0, rows), :] = first[...]
    out[pl.ds(rows, rows), :] = second[...]


def join(first, second):
    rows, span = first.shape
    return on_vmem(join_kernel, (2 * rows, span), first.dtype, "join", first, second)


def order_kernel(first, second, third, fourth, out):
    group = lax.axis_index("dp")
    for j, part in enumerate((first, second, third, fourth)):
        out[lax.bitwise_xor(group, j)] = part[...]


def order(four):
    return on_vmem(order_kernel, (4,) + four[0].shape, four[0].dtype, "order", *four)


def plane_kernel(rows, own, crossed, out):
    total = None
    for part in (own, crossed):
        terms = [part[q, rows:, :].astype(jnp.float32) for q in range(4)]
        terms = [term[: term.shape[0] // 2] + term[term.shape[0] // 2 :] for term in terms]
        found = (terms[0] + terms[1]) + (terms[2] + terms[3])
        total = found if total is None else total + found
    out[...] = unfold(total, total.shape[1] // out.shape[1])


def plane_sum(rows, shape, own, crossed):
    return on_vmem(functools.partial(plane_kernel, rows), shape, jnp.float32, "plane_sum", own, crossed)


def zeros(*shape):
    return jnp.zeros(shape, jnp.float32)


def split_copies(source, target, axis, count, sems, first):
    span = source.shape[axis] // count
    found = []
    for i in range(count):
        at = (slice(None),) * axis + (pl.ds(i * span, span),)
        found.append(pltpu.make_async_copy(source.at[at], target.at[at], sems.at[first + i]))
    return found


PARTS = 4


def validation_kernel(xv, gv, down_t, up, columns, rows_t, proj_out, xvs, gvs, downs, ups, tables, sems):
    tokens, width = xv.shape
    k2 = columns.shape[1]
    pairs = [(gv, gvs), (up, ups), (xv, xvs), (down_t, downs)]
    whole = [pltpu.make_async_copy(p[0], p[1], sems.at[i]) for i, p in enumerate(pairs)]
    parts = split_copies(columns, tables, 0, PARTS, sems, len(pairs))
    for copy in whole + parts:
        copy.start()
    whole[0].wait()
    whole[1].wait()
    back = mm(gvs[...], ups[...], NT)
    whole[2].wait()
    whole[3].wait()
    fwd = mm(xvs[...], downs[...], NT)
    mixed = zeros(2 * tokens, 2 * k2)
    span = width // PARTS
    for i in range(PARTS):
        parts[i].wait()
        cols = pl.ds(i * span, span)
        table = jnp.concatenate(two_terms(tables[cols, :]), axis=1)
        mixed = mixed + mm(jnp.concatenate([xvs[:, cols], gvs[:, cols]], axis=0), table)
    mixed = mixed[:, :k2] + mixed[:, k2:]
    inner_top = mm(back.astype(jnp.bfloat16).astype(jnp.float32), mixed[:tokens], TN, HIGHEST)
    inner_bottom = mm(fwd.astype(jnp.bfloat16).astype(jnp.float32), mixed[tokens:], TN, HIGHEST)
    inner = jnp.concatenate([inner_top, inner_bottom], axis=0)
    proj_out[...] = mm(rows_t[...], inner, NN, HIGHEST)


def prepare_kernel(lengths, x, g, down_t, up, top_out, bottom_out):
    tokens, rank = x.shape[0], up.shape[0]
    position = lax.broadcasted_iota(jnp.int32, (rank, tokens), 1)
    for left, right, out in ((g, up, top_out), (x, down_t, bottom_out)):
        turned = mm(left[...], right[...], NT).T
        begin = jnp.int32(0)
        for e in range(lengths.shape[0]):
            finish = begin + lengths[e]
            member = (position >= begin) & (position < finish)
            out[pl.ds(e * rank, rank), :] = jnp.where(member, turned, 0.0).astype(jnp.bfloat16)
            begin = finish


def validation(xv, gv, down_t, up, columns, rows_t):
    return pl.pallas_call(
        validation_kernel,
        in_specs=[ANY] * 5 + [VMEM],
        out_specs=VMEM,
        out_shape=jax.ShapeDtypeStruct((rows_t.shape[0], columns.shape[1]), jnp.float32),
        scratch_shapes=[
            *(pltpu.VMEM(a.shape, a.dtype) for a in (xv, gv, down_t, up, columns)),
            pltpu.SemaphoreType.DMA((4 + PARTS,)),
        ],
        compiler_params=pltpu.CompilerParams(vmem_limit_bytes=VMEM_LIMIT),
        cost_estimate=pl.CostEstimate(flops=10**6, bytes_accessed=10**6, transcendentals=0),
        name="validation",
    )(xv, gv, down_t, up, columns, rows_t)


def prepare(lengths, x, g, down_t, up):
    shape = jax.ShapeDtypeStruct((lengths.shape[0] * up.shape[0], x.shape[0]), jnp.bfloat16)
    return pl.pallas_call(
        prepare_kernel,
        in_specs=[SMEM] + [VMEM] * 4,
        out_specs=[VMEM] * 2,
        out_shape=[shape, shape],
        compiler_params=pltpu.CompilerParams(vmem_limit_bytes=CHUNK_LIMIT),
        cost_estimate=pl.CostEstimate(flops=10**6, bytes_accessed=10**6, transcendentals=0),
        name="prepare",
    )(lengths, x, g, down_t, up)


def accumulate(blocks, moments, slots, x, g, columns, top, bottom, update, inner):
    _, rows2, span = update.shape
    rank = (rows2 - top.shape[0]) // 2
    examples = top.shape[0] // rank
    cut = min(span, 256)
    starts = [pl.multiple_of(slots[slot_of()] * span, span) for slot_of, _ in blocks]
    tiles = [(b, half, c) for b in range(len(blocks)) for half in (0, 1) for c in range(0, span, cut)]
    sources, masks = (x, g), (top, bottom)

    def gradient(tile):
        b, half, c = tile
        cols = pl.ds(pl.multiple_of(starts[b] + c, cut), cut)
        return mm(masks[half][...], sources[half][:, cols])

    def moment(b, k, half, cols):
        ref, low, quarter = blocks[b][1](moments, k)
        parts = ref.shape[0] // 2
        found = ref[half * parts : (half + 1) * parts, low : low + quarter, cols]
        return found.astype(jnp.float32).reshape(rank, cut)

    def elementwise(tile, grad):
        b, half, c = tile
        cols = pl.ds(c, cut)
        first = 9.0 * moment(b, 0, half, cols)
        second = 999.0 * moment(b, 1, half, cols)
        shared = first * lax.rsqrt(second)
        coarse, fine = two_terms(shared)
        update[half, pl.ds(examples * rank, rank), cols] = coarse
        update[half, pl.ds((examples + 1) * rank, rank), cols] = fine
        for e in range(examples):
            piece = grad[e * rank : (e + 1) * rank]
            change = (first + piece) * lax.rsqrt(second + piece * piece) - shared
            update[half, pl.ds(e * rank, rank), cols] = change.astype(jnp.bfloat16)

    grad = gradient(tiles[0])
    for i, tile in enumerate(tiles):
        following = gradient(tiles[i + 1]) if i + 1 < len(tiles) else None
        elementwise(tile, grad)
        grad = following
        b, half, c = tile
        if c + cut == span:
            if half == 0:
                table = jnp.concatenate(two_terms(columns[pl.ds(starts[b], span), :]), axis=1)
            product = mm(update[half], table)
            inner[half] = product if b == 0 else inner[half] + product


def folded(inner, half, examples, rank, e):
    k2 = inner.shape[2] // 2
    part = pl.ds(e * rank, rank)
    total = inner[half, part, :k2] + inner[half, part, k2:]
    if e == examples:
        part = pl.ds((examples + 1) * rank, rank)
        total = total + inner[half, part, :k2] + inner[half, part, k2:]
    return total


def chunk_kernel(blocks, n_moments, slots, *refs):
    moments, refs = refs[:n_moments], refs[n_moments:]
    x, g, columns, top, bottom, out, update, inner = refs
    accumulate(blocks, moments, slots, x, g, columns, top, bottom, update, inner)
    rank = (update.shape[1] - top.shape[0]) // 2
    examples = top.shape[0] // rank
    for half in (0, 1):
        for e in range(examples + 1):
            out[half, pl.ds(e * rank, rank), :] = folded(inner, half, examples, rank, e)


def last_kernel(blocks, n_moments, n_val, n_partial, slots, *refs):
    moments, refs = refs[:n_moments], refs[n_moments:]
    x, g, columns, top, bottom, rows_t = refs[:6]
    val_parts, refs = refs[6 : 6 + n_val], refs[6 + n_val :]
    partials, refs = refs[:n_partial], refs[n_partial:]
    dirs_out, val_out, scores_out, joined, directions, update, inner = refs
    accumulate(blocks, moments, slots, x, g, columns, top, bottom, update, inner)
    rank = (update.shape[1] - top.shape[0]) // 2
    examples = top.shape[0] // rank
    k1, k2 = rows_t.shape[0], columns.shape[1]
    size = k1 * k2
    val = val_parts[0][...]
    for part in val_parts[1:]:
        val = val + part[...]
    val_dir = val * lax.rsqrt(jnp.sum(val * val) / size + epsilon)
    val_out[...] = val_dir
    rows = rows_t[...] * update_scale
    for e in range(examples + 1):
        for half in (0, 1):
            total = folded(inner, half, examples, rank, e)
            for partial in partials:
                total = total + partial[half, pl.ds(e * rank, rank), :]
            joined[pl.ds(half * rank, rank), pl.ds(e * k2, k2)] = total
    projected = mm(rows, joined[...], NN, HIGHEST)
    base = projected[:, examples * k2 :]
    projs = [projected[:, e * k2 : (e + 1) * k2] + base for e in range(examples)]

    def sums(products):
        return jnp.sum(jnp.concatenate([jnp.sum(p, axis=0, keepdims=True) for p in products], axis=0), axis=1, keepdims=True)

    scale = lax.rsqrt(sums([proj * proj for proj in projs]) / size + epsilon)
    scores = sums([proj * val_dir for proj in projs]) * scale / math.sqrt(size)
    for e in range(examples):
        directions[e] = projs[e] * scale[e : e + 1]
        scores_out[e] = scores[e, 0]
    for j in range(k1):
        dirs_out[:, pl.ds(j * k2, k2)] = directions[:, j, :]


def chunk(slots, blocks, moments, x, g, columns, top, bottom, rank, last=None):
    tokens, width = x.shape
    k2 = columns.shape[1]
    span = width // slots.shape[0]
    examples = top.shape[0] // rank
    scratch = [
        pltpu.VMEM((2, (examples + 2) * rank, span), jnp.bfloat16),
        pltpu.VMEM((2, (examples + 2) * rank, 2 * k2), jnp.float32),
    ]
    common = [SMEM] + [VMEM] * (len(moments) + 5)
    operands = [slots, *moments, x, g, columns, top, bottom]
    options = dict(
        compiler_params=pltpu.CompilerParams(vmem_limit_bytes=CHUNK_LIMIT),
        cost_estimate=pl.CostEstimate(flops=10**6, bytes_accessed=10**6, transcendentals=0),
    )
    if last is None:
        return pl.pallas_call(
            functools.partial(chunk_kernel, blocks, len(moments)),
            in_specs=common,
            out_specs=VMEM,
            out_shape=jax.ShapeDtypeStruct((2, (examples + 1) * rank, k2), jnp.float32),
            scratch_shapes=scratch,
            name="chunk",
            **options,
        )(*operands)
    rows_t, val_parts, partials = last
    k1 = rows_t.shape[0]
    return pl.pallas_call(
        functools.partial(last_kernel, blocks, len(moments), len(val_parts), len(partials)),
        in_specs=common + [VMEM] * (1 + len(val_parts) + len(partials)),
        out_specs=[VMEM, VMEM, SMEM],
        out_shape=[
            jax.ShapeDtypeStruct((examples, k1 * k2), jnp.float32),
            jax.ShapeDtypeStruct((k1, k2), jnp.float32),
            jax.ShapeDtypeStruct((examples,), jnp.float32),
        ],
        scratch_shapes=[
            pltpu.VMEM((2 * rank, (examples + 1) * k2), jnp.float32),
            pltpu.VMEM((examples, k1, k2), jnp.float32),
            *scratch,
        ],
        name="last_chunk",
        **options,
    )(*operands, rows_t, *val_parts, *partials)


def slot_at(other, hop):
    return lambda: lax.bitwise_xor(lax.axis_index("shard"), 2 * hop + other)


def ordered_block(quarter, other, hop, which, place):
    return slot_at(other, hop), lambda moments, k: (moments[which], (2 * place + k) * quarter, quarter)


def paired_block(quarter, other, which):
    return slot_at(other, 0), lambda moments, k: (moments[2 * which + k], 0, quarter)


def gathered_block(quarter, b):
    return lambda: b, lambda moments, k: (moments[k].at[b], 0, quarter)


def exchange(value, axis, bits):
    size = lax.axis_size(axis)
    return lax.ppermute(value, axis, [(i, i ^ bits) for i in range(size)])


def body(
    training_inputs,
    training_cotangents,
    validation_inputs,
    validation_cotangents,
    adapter_down,
    adapter_up,
    adam_first_moment,
    adam_second_moment,
    slot_block_index,
    example_lengths,
    projection_rows,
    projection_columns,
):
    groups = lax.axis_size("dp")
    shards = lax.axis_size("shard")
    rank = adapter_up.shape[0]
    quarter = 2 * rank // groups
    stepwise = groups == 4 and shards == 8
    rows_t = projection_rows.T
    own = [m.reshape(groups, quarter, -1) for m in (adam_first_moment, adam_second_moment)]
    train = (training_inputs, training_cotangents)
    if stepwise:
        piece = cut_piece(*own)
        sibling = [exchange(m, "shard", 1) for m in own]
        far = [exchange(piece, "shard", 2 * hop) for hop in (1, 2, 3)]
        validation_inputs, _ = lax.optimization_barrier((validation_inputs, piece))
    down_t = adapter_down.T
    val_part = validation(
        validation_inputs, validation_cotangents, down_t, adapter_up, projection_columns, rows_t
    )
    lengths, val_part = lax.optimization_barrier((example_lengths[0, 0], val_part))
    top, bottom = prepare(lengths, *train, down_t, adapter_up)
    if stepwise:
        val_part, *sibling, far[0], far[1] = lax.optimization_barrier((val_part, *sibling, far[0], far[1]))
        packed = pack(far[0], val_part)
        near = [packed] + [exchange(packed, "dp", bits) for bits in (1, 2, 3)]
        *arrived, top, bottom = lax.optimization_barrier((*far[1:], *near, top, bottom))
        rest = join(*arrived[:2])
        four = [rest] + [exchange(rest, "dp", bits) for bits in (1, 2, 3)]
        one = order(arrived[2:])
        one, top, bottom = lax.optimization_barrier((one, top, bottom))
        one_crossed = exchange(one, "shard", 1)
        operands = (*train, projection_columns, top, bottom, rank)
        slots = slot_block_index
        partials = [chunk(slots, [paired_block(quarter, i, i) for i in (0, 1)], own + sibling, *operands)]
        partials[0], one_crossed = lax.optimization_barrier((partials[0], one_crossed))
        total = plane_sum(2 * quarter, val_part.shape, one, one_crossed)
        total, one_crossed = lax.optimization_barrier((total, one_crossed))
        other = exchange(total, "shard", 2)
        partials.append(
            chunk(slots, [ordered_block(quarter, i, 1, i, 0) for i in (0, 1)], [one, one_crossed], *operands)
        )
        partials[1], other, *four = lax.optimization_barrier((partials[1], other, *four))
        total = total + other
        both = order(four)
        total, both = lax.optimization_barrier((total, both))
        val_parts = [total, exchange(total, "shard", 4)]
        both_crossed = exchange(both, "shard", 1)
        partials.append(chunk(slots, [ordered_block(quarter, 0, 2 + i, 0, i) for i in (0, 1)], [both], *operands))
        dirs, val_dir, scores = chunk(
            slots,
            [ordered_block(quarter, 1, 2 + i, 0, i) for i in (0, 1)],
            [both_crossed],
            *operands,
            last=(rows_t, val_parts, partials),
        )
    else:
        operands = (*train, projection_columns, top, bottom, rank)
        gathered = [lax.all_gather(m, "shard", axis=0, tiled=False) for m in own]
        val_sum = lax.psum(val_part, ("dp", "shard"))
        dirs, val_dir, scores = chunk(
            slot_block_index,
            [gathered_block(quarter, b) for b in range(shards)],
            gathered,
            *operands,
            last=(rows_t, [val_sum], []),
        )
    return (
        dirs.reshape(1, 1, dirs.shape[0], -1),
        val_dir.reshape(-1),
        scores[None, None],
    )


def solution(mesh):
    return jax.shard_map(
        body,
        mesh=mesh,
        in_specs=(
            P(("dp", "shard"), None),
            P(("dp", "shard"), None),
            P(("dp", "shard"), None),
            P(("dp", "shard"), None),
            P(),
            P(),
            P("shard", None, None),
            P("shard", None, None),
            P(),
            P("dp", "shard", None),
            P(),
            P(),
        ),
        out_specs=(P("dp", "shard", None, None), P(), P("dp", "shard", None)),
        check_vma=False,
    )
```

```python
import functools
import math

import jax
import jax.numpy as jnp
from jax import lax
from jax.experimental import pallas as pl
from jax.experimental.pallas import tpu as pltpu
from jax.sharding import PartitionSpec as P

epsilon = 1e-06
update_scale = 0.1 / math.sqrt(0.001)
HIGHEST = lax.Precision.HIGHEST
NN = (((1,), (0,)), ((), ()))
TN = (((0,), (0,)), ((), ()))
NT = (((1,), (1,)), ((), ()))
VMEM_LIMIT = 60 * 1024 * 1024
CHUNK_LIMIT = 24 * 1024 * 1024
ANY = pl.BlockSpec(memory_space=pl.ANY)
SMEM = pl.BlockSpec(memory_space=pltpu.SMEM)
VMEM = pl.BlockSpec(memory_space=pltpu.VMEM)


def mm(a, b, dims=NN, precision=None):
    return lax.dot_general(a, b, dims, precision=precision, preferred_element_type=jnp.float32)


def two_terms(exact):
    coarse = exact.astype(jnp.bfloat16)
    fine = (exact - coarse.astype(jnp.float32)).astype(jnp.bfloat16)
    return coarse, fine


def cut_kernel(first, second, out, sems):
    group = lax.axis_index("dp")
    quarter = first.shape[1]
    copies = [
        pltpu.make_async_copy(source.at[group], out.at[pl.ds(i * quarter, quarter)], sems.at[i])
        for i, source in enumerate((first, second))
    ]
    for copy in copies:
        copy.start()
    for copy in copies:
        copy.wait()


def cut_piece(first, second):
    return pl.pallas_call(
        cut_kernel,
        in_specs=[ANY, ANY],
        out_specs=VMEM,
        out_shape=jax.ShapeDtypeStruct((2 * first.shape[1], first.shape[2]), first.dtype),
        scratch_shapes=[pltpu.SemaphoreType.DMA((2,))],
        compiler_params=pltpu.CompilerParams(vmem_limit_bytes=VMEM_LIMIT),
        name="cut_piece",
    )(first, second)


def fold(tall, times):
    rows = tall.shape[0] // times
    return jnp.concatenate([tall[i * rows : (i + 1) * rows] for i in range(times)], axis=1)


def unfold(wide, times):
    cols = wide.shape[1] // times
    return jnp.concatenate([wide[:, i * cols : (i + 1) * cols] for i in range(times)], axis=0)


def on_vmem(kernel, shape, dtype, name, *operands):
    return pl.pallas_call(
        kernel,
        in_specs=[VMEM] * len(operands),
        out_specs=VMEM,
        out_shape=jax.ShapeDtypeStruct(shape, dtype),
        compiler_params=pltpu.CompilerParams(vmem_limit_bytes=CHUNK_LIMIT),
        name=name,
    )(*operands)


def pack_kernel(first, second, val, out):
    rows = first.shape[0]
    out[pl.ds(0, rows), :] = first[...]
    out[pl.ds(rows, rows), :] = second[...]
    wide = fold(val[...], out.shape[1] // val.shape[1])
    coarse = wide.astype(jnp.bfloat16).astype(jnp.float32)
    terms = jnp.concatenate([coarse, wide - coarse], axis=0)
    out[pl.ds(2 * rows, terms.shape[0]), :] = terms.astype(jnp.bfloat16)


def pack(first, second, val):
    rows, span = first.shape
    return on_vmem(pack_kernel, (2 * rows + 2 * val.size // span, span), first.dtype, "pack", first, second, val)


def order_kernel(first, second, third, fourth, out):
    group = lax.axis_index("dp")
    for j, part in enumerate((first, second, third, fourth)):
        out[lax.bitwise_xor(group, j)] = part[...]


def order(four):
    return on_vmem(order_kernel, (4,) + four[0].shape, four[0].dtype, "order", *four)


def plane_kernel(rows, own, crossed, out):
    total = None
    for part in (own, crossed):
        terms = [part[q, rows:, :].astype(jnp.float32) for q in range(4)]
        terms = [term[: term.shape[0] // 2] + term[term.shape[0] // 2 :] for term in terms]
        found = (terms[0] + terms[1]) + (terms[2] + terms[3])
        total = found if total is None else total + found
    out[...] = unfold(total, total.shape[1] // out.shape[1])


def plane_sum(rows, shape, own, crossed):
    return on_vmem(functools.partial(plane_kernel, rows), shape, jnp.float32, "plane_sum", own, crossed)


def zeros(*shape):
    return jnp.zeros(shape, jnp.float32)


def split_copies(source, target, axis, count, sems, first):
    span = source.shape[axis] // count
    found = []
    for i in range(count):
        at = (slice(None),) * axis + (pl.ds(i * span, span),)
        found.append(pltpu.make_async_copy(source.at[at], target.at[at], sems.at[first + i]))
    return found


PARTS = 4


def validation_kernel(xv, gv, down_t, up, columns, rows_t, proj_out, xvs, gvs, downs, ups, tables, sems):
    tokens, width = xv.shape
    k2 = columns.shape[1]
    pairs = [(gv, gvs), (up, ups), (xv, xvs), (down_t, downs)]
    whole = [pltpu.make_async_copy(p[0], p[1], sems.at[i]) for i, p in enumerate(pairs)]
    parts = split_copies(columns, tables, 0, PARTS, sems, len(pairs))
    for copy in whole + parts:
        copy.start()
    whole[0].wait()
    whole[1].wait()
    back = mm(gvs[...], ups[...], NT)
    whole[2].wait()
    whole[3].wait()
    fwd = mm(xvs[...], downs[...], NT)
    mixed = zeros(2 * tokens, 2 * k2)
    span = width // PARTS
    for i in range(PARTS):
        parts[i].wait()
        cols = pl.ds(i * span, span)
        table = jnp.concatenate(two_terms(tables[cols, :]), axis=1)
        mixed = mixed + mm(jnp.concatenate([xvs[:, cols], gvs[:, cols]], axis=0), table)
    mixed = mixed[:, :k2] + mixed[:, k2:]
    inner_top = mm(back.astype(jnp.bfloat16).astype(jnp.float32), mixed[:tokens], TN, HIGHEST)
    inner_bottom = mm(fwd.astype(jnp.bfloat16).astype(jnp.float32), mixed[tokens:], TN, HIGHEST)
    inner = jnp.concatenate([inner_top, inner_bottom], axis=0)
    proj_out[...] = mm(rows_t[...], inner, NN, HIGHEST)


def prepare_kernel(lengths, x, g, down_t, up, top_out, bottom_out):
    tokens, rank = x.shape[0], up.shape[0]
    position = lax.broadcasted_iota(jnp.int32, (rank, tokens), 1)
    for left, right, out in ((g, up, top_out), (x, down_t, bottom_out)):
        turned = mm(left[...], right[...], NT).T
        begin = jnp.int32(0)
        for e in range(lengths.shape[0]):
            finish = begin + lengths[e]
            member = (position >= begin) & (position < finish)
            out[pl.ds(e * rank, rank), :] = jnp.where(member, turned, 0.0).astype(jnp.bfloat16)
            begin = finish


def validation(xv, gv, down_t, up, columns, rows_t):
    return pl.pallas_call(
        validation_kernel,
        in_specs=[ANY] * 5 + [VMEM],
        out_specs=VMEM,
        out_shape=jax.ShapeDtypeStruct((rows_t.shape[0], columns.shape[1]), jnp.float32),
        scratch_shapes=[
            *(pltpu.VMEM(a.shape, a.dtype) for a in (xv, gv, down_t, up, columns)),
            pltpu.SemaphoreType.DMA((4 + PARTS,)),
        ],
        compiler_params=pltpu.CompilerParams(vmem_limit_bytes=VMEM_LIMIT),
        cost_estimate=pl.CostEstimate(flops=10**6, bytes_accessed=10**6, transcendentals=0),
        name="validation",
    )(xv, gv, down_t, up, columns, rows_t)


def prepare(lengths, x, g, down_t, up):
    shape = jax.ShapeDtypeStruct((lengths.shape[0] * up.shape[0], x.shape[0]), jnp.bfloat16)
    return pl.pallas_call(
        prepare_kernel,
        in_specs=[SMEM] + [VMEM] * 4,
        out_specs=[VMEM] * 2,
        out_shape=[shape, shape],
        compiler_params=pltpu.CompilerParams(vmem_limit_bytes=CHUNK_LIMIT),
        cost_estimate=pl.CostEstimate(flops=10**6, bytes_accessed=10**6, transcendentals=0),
        name="prepare",
    )(lengths, x, g, down_t, up)


def accumulate(blocks, moments, slots, x, g, columns, top, bottom, update, inner):
    _, rows2, span = update.shape
    rank = (rows2 - top.shape[0]) // 2
    examples = top.shape[0] // rank
    cut = min(span, 256)
    starts = [pl.multiple_of(slots[slot_of()] * span, span) for slot_of, _ in blocks]
    tiles = [(b, half, c) for b in range(len(blocks)) for half in (0, 1) for c in range(0, span, cut)]
    sources, masks = (x, g), (top, bottom)

    def gradient(tile):
        b, half, c = tile
        cols = pl.ds(pl.multiple_of(starts[b] + c, cut), cut)
        return mm(masks[half][...], sources[half][:, cols])

    def moment(b, k, half, cols):
        ref, low, quarter = blocks[b][1](moments, k)
        parts = ref.shape[0] // 2
        found = ref[half * parts : (half + 1) * parts, low : low + quarter, cols]
        return found.astype(jnp.float32).reshape(rank, cut)

    def elementwise(tile, grad):
        b, half, c = tile
        cols = pl.ds(c, cut)
        first = 9.0 * moment(b, 0, half, cols)
        second = 999.0 * moment(b, 1, half, cols)
        shared = first * lax.rsqrt(second)
        coarse, fine = two_terms(shared)
        update[half, pl.ds(examples * rank, rank), cols] = coarse
        update[half, pl.ds((examples + 1) * rank, rank), cols] = fine
        for e in range(examples):
            piece = grad[e * rank : (e + 1) * rank]
            change = (first + piece) * lax.rsqrt(second + piece * piece) - shared
            update[half, pl.ds(e * rank, rank), cols] = change.astype(jnp.bfloat16)

    grad = gradient(tiles[0])
    for i, tile in enumerate(tiles):
        following = gradient(tiles[i + 1]) if i + 1 < len(tiles) else None
        elementwise(tile, grad)
        grad = following
        b, half, c = tile
        if c + cut == span:
            if half == 0:
                table = jnp.concatenate(two_terms(columns[pl.ds(starts[b], span), :]), axis=1)
            product = mm(update[half], table)
            inner[half] = product if b == 0 else inner[half] + product


def folded(inner, half, examples, rank, e):
    k2 = inner.shape[2] // 2
    part = pl.ds(e * rank, rank)
    total = inner[half, part, :k2] + inner[half, part, k2:]
    if e == examples:
        part = pl.ds((examples + 1) * rank, rank)
        total = total + inner[half, part, :k2] + inner[half, part, k2:]
    return total


def chunk_kernel(blocks, n_moments, slots, *refs):
    moments, refs = refs[:n_moments], refs[n_moments:]
    x, g, columns, top, bottom, out, update, inner = refs
    accumulate(blocks, moments, slots, x, g, columns, top, bottom, update, inner)
    rank = (update.shape[1] - top.shape[0]) // 2
    examples = top.shape[0] // rank
    for half in (0, 1):
        for e in range(examples + 1):
            out[half, pl.ds(e * rank, rank), :] = folded(inner, half, examples, rank, e)


def last_kernel(blocks, n_moments, n_val, n_partial, slots, *refs):
    moments, refs = refs[:n_moments], refs[n_moments:]
    x, g, columns, top, bottom, rows_t = refs[:6]
    val_parts, refs = refs[6 : 6 + n_val], refs[6 + n_val :]
    partials, refs = refs[:n_partial], refs[n_partial:]
    dirs_out, val_out, scores_out, joined, directions, update, inner = refs
    accumulate(blocks, moments, slots, x, g, columns, top, bottom, update, inner)
    rank = (update.shape[1] - top.shape[0]) // 2
    examples = top.shape[0] // rank
    k1, k2 = rows_t.shape[0], columns.shape[1]
    size = k1 * k2
    val = val_parts[0][...]
    for part in val_parts[1:]:
        val = val + part[...]
    val_dir = val * lax.rsqrt(jnp.sum(val * val) / size + epsilon)
    val_out[...] = val_dir
    rows = rows_t[...] * update_scale
    for e in range(examples + 1):
        for half in (0, 1):
            total = folded(inner, half, examples, rank, e)
            for partial in partials:
                total = total + partial[half, pl.ds(e * rank, rank), :]
            joined[pl.ds(half * rank, rank), pl.ds(e * k2, k2)] = total
    projected = mm(rows, joined[...], NN, HIGHEST)
    base = projected[:, examples * k2 :]
    projs = [projected[:, e * k2 : (e + 1) * k2] + base for e in range(examples)]

    def sums(products):
        return jnp.sum(jnp.concatenate([jnp.sum(p, axis=0, keepdims=True) for p in products], axis=0), axis=1, keepdims=True)

    scale = lax.rsqrt(sums([proj * proj for proj in projs]) / size + epsilon)
    scores = sums([proj * val_dir for proj in projs]) * scale / math.sqrt(size)
    for e in range(examples):
        directions[e] = projs[e] * scale[e : e + 1]
        scores_out[e] = scores[e, 0]
    for j in range(k1):
        dirs_out[:, pl.ds(j * k2, k2)] = directions[:, j, :]


def chunk(slots, blocks, moments, x, g, columns, top, bottom, rank, last=None):
    tokens, width = x.shape
    k2 = columns.shape[1]
    span = width // slots.shape[0]
    examples = top.shape[0] // rank
    scratch = [
        pltpu.VMEM((2, (examples + 2) * rank, span), jnp.bfloat16),
        pltpu.VMEM((2, (examples + 2) * rank, 2 * k2), jnp.float32),
    ]
    common = [SMEM] + [VMEM] * (len(moments) + 5)
    operands = [slots, *moments, x, g, columns, top, bottom]
    options = dict(
        compiler_params=pltpu.CompilerParams(vmem_limit_bytes=CHUNK_LIMIT),
        cost_estimate=pl.CostEstimate(flops=10**6, bytes_accessed=10**6, transcendentals=0),
    )
    if last is None:
        return pl.pallas_call(
            functools.partial(chunk_kernel, blocks, len(moments)),
            in_specs=common,
            out_specs=VMEM,
            out_shape=jax.ShapeDtypeStruct((2, (examples + 1) * rank, k2), jnp.float32),
            scratch_shapes=scratch,
            name="chunk",
            **options,
        )(*operands)
    rows_t, val_parts, partials = last
    k1 = rows_t.shape[0]
    return pl.pallas_call(
        functools.partial(last_kernel, blocks, len(moments), len(val_parts), len(partials)),
        in_specs=common + [VMEM] * (1 + len(val_parts) + len(partials)),
        out_specs=[VMEM, VMEM, SMEM],
        out_shape=[
            jax.ShapeDtypeStruct((examples, k1 * k2), jnp.float32),
            jax.ShapeDtypeStruct((k1, k2), jnp.float32),
            jax.ShapeDtypeStruct((examples,), jnp.float32),
        ],
        scratch_shapes=[
            pltpu.VMEM((2 * rank, (examples + 1) * k2), jnp.float32),
            pltpu.VMEM((examples, k1, k2), jnp.float32),
            *scratch,
        ],
        name="last_chunk",
        **options,
    )(*operands, rows_t, *val_parts, *partials)


def slot_at(other, hop):
    return lambda: lax.bitwise_xor(lax.axis_index("shard"), 2 * hop + other)


def ordered_block(quarter, other, hop, which, place):
    return slot_at(other, hop), lambda moments, k: (moments[which], (2 * place + k) * quarter, quarter)


def paired_block(quarter, other, which):
    return slot_at(other, 0), lambda moments, k: (moments[2 * which + k], 0, quarter)


def gathered_block(quarter, b):
    return lambda: b, lambda moments, k: (moments[k].at[b], 0, quarter)


def exchange(value, axis, bits):
    size = lax.axis_size(axis)
    return lax.ppermute(value, axis, [(i, i ^ bits) for i in range(size)])


def body(
    training_inputs,
    training_cotangents,
    validation_inputs,
    validation_cotangents,
    adapter_down,
    adapter_up,
    adam_first_moment,
    adam_second_moment,
    slot_block_index,
    example_lengths,
    projection_rows,
    projection_columns,
):
    groups = lax.axis_size("dp")
    shards = lax.axis_size("shard")
    rank = adapter_up.shape[0]
    quarter = 2 * rank // groups
    stepwise = groups == 4 and shards == 8
    rows_t = projection_rows.T
    own = [m.reshape(groups, quarter, -1) for m in (adam_first_moment, adam_second_moment)]
    train = (training_inputs, training_cotangents)
    if stepwise:
        piece = cut_piece(*own)
        sibling = [exchange(m, "shard", 1) for m in own]
        far = [exchange(piece, "shard", 2 * hop) for hop in (1, 2, 3)]
        validation_inputs, _ = lax.optimization_barrier((validation_inputs, piece))
    down_t = adapter_down.T
    val_part = validation(
        validation_inputs, validation_cotangents, down_t, adapter_up, projection_columns, rows_t
    )
    lengths, val_part = lax.optimization_barrier((example_lengths[0, 0], val_part))
    top, bottom = prepare(lengths, *train, down_t, adapter_up)
    if stepwise:
        val_part, *sibling, far[0], far[1] = lax.optimization_barrier((val_part, *sibling, far[0], far[1]))
        packed = pack(far[0], far[1], val_part)
        near = [packed] + [exchange(packed, "dp", bits) for bits in (1, 2, 3)]
        operands = (*train, projection_columns, top, bottom, rank)
        slots = slot_block_index
        first = chunk(slots, [paired_block(quarter, i, i) for i in (0, 1)], own + sibling, *operands)
        first, last_far, *near = lax.optimization_barrier((first, far[2], *near))
        four = [last_far] + [exchange(last_far, "dp", bits) for bits in (1, 2, 3)]
        one = order(near)
        one_crossed = exchange(one, "shard", 1)
        second = chunk(slots, [ordered_block(quarter, 0, 1 + i, 0, i) for i in (0, 1)], [one], *operands)
        second, one_crossed, *four = lax.optimization_barrier((second, one_crossed, *four))
        total = plane_sum(4 * quarter, val_part.shape, one, one_crossed)
        both = order(four)
        total, both, one_crossed = lax.optimization_barrier((total, both, one_crossed))
        other = exchange(total, "shard", 2)
        both_crossed = exchange(both, "shard", 1)
        third = chunk(slots, [ordered_block(quarter, 1, 1 + i, 0, i) for i in (0, 1)], [one_crossed], *operands)
        third, other = lax.optimization_barrier((third, other))
        total = total + other
        val_parts = [total, exchange(total, "shard", 4)]
        dirs, val_dir, scores = chunk(
            slots,
            [ordered_block(quarter, i, 3, i, 0) for i in (0, 1)],
            [both, both_crossed],
            *operands,
            last=(rows_t, val_parts, [first, second, third]),
        )
    else:
        operands = (*train, projection_columns, top, bottom, rank)
        gathered = [lax.all_gather(m, "shard", axis=0, tiled=False) for m in own]
        val_sum = lax.psum(val_part, ("dp", "shard"))
        dirs, val_dir, scores = chunk(
            slot_block_index,
            [gathered_block(quarter, b) for b in range(shards)],
            gathered,
            *operands,
            last=(rows_t, [val_sum], []),
        )
    return (
        dirs.reshape(1, 1, dirs.shape[0], -1),
        val_dir.reshape(-1),
        scores[None, None],
    )


def solution(mesh):
    return jax.shard_map(
        body,
        mesh=mesh,
        in_specs=(
            P(("dp", "shard"), None),
            P(("dp", "shard"), None),
            P(("dp", "shard"), None),
            P(("dp", "shard"), None),
            P(),
            P(),
            P("shard", None, None),
            P("shard", None, None),
            P(),
            P("dp", "shard", None),
            P(),
            P(),
        ),
        out_specs=(P("dp", "shard", None, None), P(), P("dp", "shard", None)),
        check_vma=False,
    )
```

```python
import functools
import math

import jax
import jax.numpy as jnp
from jax import lax
from jax.experimental import pallas as pl
from jax.experimental.pallas import tpu as pltpu
from jax.sharding import PartitionSpec as P

epsilon = 1e-06
update_scale = 0.1 / math.sqrt(0.001)
HIGHEST = lax.Precision.HIGHEST
NN = (((1,), (0,)), ((), ()))
TN = (((0,), (0,)), ((), ()))
NT = (((1,), (1,)), ((), ()))
VMEM_LIMIT = 60 * 1024 * 1024
VALIDATION_LIMIT = 57 * 1024 * 1024
CHUNK_LIMIT = 24 * 1024 * 1024
ANY = pl.BlockSpec(memory_space=pl.ANY)
SMEM = pl.BlockSpec(memory_space=pltpu.SMEM)
VMEM = pl.BlockSpec(memory_space=pltpu.VMEM)


def mm(a, b, dims=NN, precision=None):
    return lax.dot_general(a, b, dims, precision=precision, preferred_element_type=jnp.float32)


def two_terms(exact):
    coarse = exact.astype(jnp.bfloat16)
    fine = (exact - coarse.astype(jnp.float32)).astype(jnp.bfloat16)
    return coarse, fine


def cut_kernel(first, second, out, sems):
    group = lax.axis_index("dp")
    quarter = first.shape[1]
    copies = [
        pltpu.make_async_copy(source.at[group], out.at[pl.ds(i * quarter, quarter)], sems.at[i])
        for i, source in enumerate((first, second))
    ]
    for copy in copies:
        copy.start()
    for copy in copies:
        copy.wait()


def cut_piece(first, second):
    return pl.pallas_call(
        cut_kernel,
        in_specs=[ANY, ANY],
        out_specs=VMEM,
        out_shape=jax.ShapeDtypeStruct((2 * first.shape[1], first.shape[2]), first.dtype),
        scratch_shapes=[pltpu.SemaphoreType.DMA((2,))],
        compiler_params=pltpu.CompilerParams(vmem_limit_bytes=VMEM_LIMIT),
        name="cut_piece",
    )(first, second)


def fold(tall, times):
    rows = tall.shape[0] // times
    return jnp.concatenate([tall[i * rows : (i + 1) * rows] for i in range(times)], axis=1)


def unfold(wide, times):
    cols = wide.shape[1] // times
    return jnp.concatenate([wide[:, i * cols : (i + 1) * cols] for i in range(times)], axis=0)


def on_vmem(kernel, shape, dtype, name, *operands):
    return pl.pallas_call(
        kernel,
        in_specs=[VMEM] * len(operands),
        out_specs=VMEM,
        out_shape=jax.ShapeDtypeStruct(shape, dtype),
        compiler_params=pltpu.CompilerParams(vmem_limit_bytes=CHUNK_LIMIT),
        name=name,
    )(*operands)


def pack_kernel(piece, val, out):
    rows = piece.shape[0]
    out[pl.ds(0, rows), :] = piece[...]
    wide = fold(val[...], out.shape[1] // val.shape[1])
    coarse = wide.astype(jnp.bfloat16).astype(jnp.float32)
    terms = jnp.concatenate([coarse, wide - coarse], axis=0)
    out[pl.ds(rows, terms.shape[0]), :] = terms.astype(jnp.bfloat16)


def pack(piece, val):
    rows, span = piece.shape
    return on_vmem(pack_kernel, (rows + 2 * val.size // span, span), piece.dtype, "pack", piece, val)


def join_kernel(first, second, out):
    rows = first.shape[0]
    out[pl.ds(0, rows), :] = first[...]
    out[pl.ds(rows, rows), :] = second[...]


def join(first, second):
    rows, span = first.shape
    return on_vmem(join_kernel, (2 * rows, span), first.dtype, "join", first, second)


def order_kernel(first, second, third, fourth, out):
    group = lax.axis_index("dp")
    for j, part in enumerate((first, second, third, fourth)):
        out[lax.bitwise_xor(group, j)] = part[...]


def order(four):
    return on_vmem(order_kernel, (4,) + four[0].shape, four[0].dtype, "order", *four)


def plane_kernel(rows, own, crossed, out):
    total = None
    for part in (own, crossed):
        terms = [part[q, rows:, :].astype(jnp.float32) for q in range(4)]
        terms = [term[: term.shape[0] // 2] + term[term.shape[0] // 2 :] for term in terms]
        found = (terms[0] + terms[1]) + (terms[2] + terms[3])
        total = found if total is None else total + found
    out[...] = unfold(total, total.shape[1] // out.shape[1])


def plane_sum(rows, shape, own, crossed):
    return on_vmem(functools.partial(plane_kernel, rows), shape, jnp.float32, "plane_sum", own, crossed)


def zeros(*shape):
    return jnp.zeros(shape, jnp.float32)


def split_copies(source, target, axis, count, sems, first):
    span = source.shape[axis] // count
    found = []
    for i in range(count):
        at = (slice(None),) * axis + (pl.ds(i * span, span),)
        found.append(pltpu.make_async_copy(source.at[at], target.at[at], sems.at[first + i]))
    return found


PARTS = 4


def validation_kernel(xv, gv, down_t, up, columns, rows_t, proj_out, xvs, gvs, downs, ups, tables, sems):
    tokens, width = xv.shape
    k2 = columns.shape[1]
    pairs = [(gv, gvs), (up, ups), (xv, xvs), (down_t, downs)]
    whole = [pltpu.make_async_copy(p[0], p[1], sems.at[i]) for i, p in enumerate(pairs)]
    parts = split_copies(columns, tables, 0, PARTS, sems, len(pairs))
    for copy in whole + parts:
        copy.start()
    whole[0].wait()
    whole[1].wait()
    back = mm(gvs[...], ups[...], NT)
    whole[2].wait()
    whole[3].wait()
    fwd = mm(xvs[...], downs[...], NT)
    mixed = zeros(2 * tokens, 2 * k2)
    span = width // PARTS
    for i in range(PARTS):
        parts[i].wait()
        cols = pl.ds(i * span, span)
        table = jnp.concatenate(two_terms(tables[cols, :]), axis=1)
        mixed = mixed + mm(jnp.concatenate([xvs[:, cols], gvs[:, cols]], axis=0), table)
    mixed = mixed[:, :k2] + mixed[:, k2:]
    inner_top = mm(back.astype(jnp.bfloat16).astype(jnp.float32), mixed[:tokens], TN, HIGHEST)
    inner_bottom = mm(fwd.astype(jnp.bfloat16).astype(jnp.float32), mixed[tokens:], TN, HIGHEST)
    inner = jnp.concatenate([inner_top, inner_bottom], axis=0)
    proj_out[...] = mm(rows_t[...], inner, NN, HIGHEST)


def prepare_kernel(lengths, x, g, down_t, up, top_out, bottom_out):
    tokens, rank = x.shape[0], up.shape[0]
    position = lax.broadcasted_iota(jnp.int32, (rank, tokens), 1)
    for left, right, out in ((g, up, top_out), (x, down_t, bottom_out)):
        turned = mm(left[...], right[...], NT).T
        begin = jnp.int32(0)
        for e in range(lengths.shape[0]):
            finish = begin + lengths[e]
            member = (position >= begin) & (position < finish)
            out[pl.ds(e * rank, rank), :] = jnp.where(member, turned, 0.0).astype(jnp.bfloat16)
            begin = finish


def validation(xv, gv, down_t, up, columns, rows_t):
    return pl.pallas_call(
        validation_kernel,
        in_specs=[ANY] * 5 + [VMEM],
        out_specs=VMEM,
        out_shape=jax.ShapeDtypeStruct((rows_t.shape[0], columns.shape[1]), jnp.float32),
        scratch_shapes=[
            *(pltpu.VMEM(a.shape, a.dtype) for a in (xv, gv, down_t, up, columns)),
            pltpu.SemaphoreType.DMA((4 + PARTS,)),
        ],
        compiler_params=pltpu.CompilerParams(vmem_limit_bytes=VALIDATION_LIMIT),
        cost_estimate=pl.CostEstimate(flops=10**6, bytes_accessed=10**6, transcendentals=0),
        name="validation",
    )(xv, gv, down_t, up, columns, rows_t)


def prepare(lengths, x, g, down_t, up):
    shape = jax.ShapeDtypeStruct((lengths.shape[0] * up.shape[0], x.shape[0]), jnp.bfloat16)
    return pl.pallas_call(
        prepare_kernel,
        in_specs=[SMEM] + [VMEM] * 4,
        out_specs=[VMEM] * 2,
        out_shape=[shape, shape],
        compiler_params=pltpu.CompilerParams(vmem_limit_bytes=CHUNK_LIMIT),
        cost_estimate=pl.CostEstimate(flops=10**6, bytes_accessed=10**6, transcendentals=0),
        name="prepare",
    )(lengths, x, g, down_t, up)


def accumulate(blocks, moments, slots, x, g, columns, top, bottom, update, inner):
    _, rows2, span = update.shape
    rank = (rows2 - top.shape[0]) // 2
    examples = top.shape[0] // rank
    cut = min(span, 256)
    starts = [pl.multiple_of(slots[slot_of()] * span, span) for slot_of, _ in blocks]
    tiles = [(b, half, c) for b in range(len(blocks)) for half in (0, 1) for c in range(0, span, cut)]
    sources, masks = (x, g), (top, bottom)

    def gradient(tile):
        b, half, c = tile
        cols = pl.ds(pl.multiple_of(starts[b] + c, cut), cut)
        return mm(masks[half][...], sources[half][:, cols])

    def moment(b, k, half, cols):
        ref, low, quarter = blocks[b][1](moments, k)
        parts = ref.shape[0] // 2
        found = ref[half * parts : (half + 1) * parts, low : low + quarter, cols]
        return found.astype(jnp.float32).reshape(rank, cut)

    def elementwise(tile, grad):
        b, half, c = tile
        cols = pl.ds(c, cut)
        first = 9.0 * moment(b, 0, half, cols)
        second = 999.0 * moment(b, 1, half, cols)
        shared = first * lax.rsqrt(second)
        coarse, fine = two_terms(shared)
        update[half, pl.ds(examples * rank, rank), cols] = coarse
        update[half, pl.ds((examples + 1) * rank, rank), cols] = fine
        for e in range(examples):
            piece = grad[e * rank : (e + 1) * rank]
            change = (first + piece) * lax.rsqrt(second + piece * piece) - shared
            update[half, pl.ds(e * rank, rank), cols] = change.astype(jnp.bfloat16)

    grad = gradient(tiles[0])
    for i, tile in enumerate(tiles):
        following = gradient(tiles[i + 1]) if i + 1 < len(tiles) else None
        elementwise(tile, grad)
        grad = following
        b, half, c = tile
        if c + cut == span:
            if half == 0:
                table = jnp.concatenate(two_terms(columns[pl.ds(starts[b], span), :]), axis=1)
            product = mm(update[half], table)
            inner[half] = product if b == 0 else inner[half] + product


def folded(inner, half, examples, rank, e):
    k2 = inner.shape[2] // 2
    part = pl.ds(e * rank, rank)
    total = inner[half, part, :k2] + inner[half, part, k2:]
    if e == examples:
        part = pl.ds((examples + 1) * rank, rank)
        total = total + inner[half, part, :k2] + inner[half, part, k2:]
    return total


def chunk_kernel(blocks, n_moments, slots, *refs):
    moments, refs = refs[:n_moments], refs[n_moments:]
    x, g, columns, top, bottom, out, update, inner = refs
    accumulate(blocks, moments, slots, x, g, columns, top, bottom, update, inner)
    rank = (update.shape[1] - top.shape[0]) // 2
    examples = top.shape[0] // rank
    for half in (0, 1):
        for e in range(examples + 1):
            out[half, pl.ds(e * rank, rank), :] = folded(inner, half, examples, rank, e)


def last_kernel(blocks, n_moments, n_val, n_partial, slots, *refs):
    moments, refs = refs[:n_moments], refs[n_moments:]
    x, g, columns, top, bottom, rows_t = refs[:6]
    val_parts, refs = refs[6 : 6 + n_val], refs[6 + n_val :]
    partials, refs = refs[:n_partial], refs[n_partial:]
    dirs_out, val_out, scores_out, joined, directions, update, inner = refs
    accumulate(blocks, moments, slots, x, g, columns, top, bottom, update, inner)
    rank = (update.shape[1] - top.shape[0]) // 2
    examples = top.shape[0] // rank
    k1, k2 = rows_t.shape[0], columns.shape[1]
    size = k1 * k2
    val = val_parts[0][...]
    for part in val_parts[1:]:
        val = val + part[...]
    val_dir = val * lax.rsqrt(jnp.sum(val * val) / size + epsilon)
    val_out[...] = val_dir
    rows = rows_t[...] * update_scale
    for e in range(examples + 1):
        for half in (0, 1):
            total = folded(inner, half, examples, rank, e)
            for partial in partials:
                total = total + partial[half, pl.ds(e * rank, rank), :]
            joined[pl.ds(half * rank, rank), pl.ds(e * k2, k2)] = total
    projected = mm(rows, joined[...], NN, HIGHEST)
    base = projected[:, examples * k2 :]
    projs = [projected[:, e * k2 : (e + 1) * k2] + base for e in range(examples)]

    def sums(products):
        return jnp.sum(jnp.concatenate([jnp.sum(p, axis=0, keepdims=True) for p in products], axis=0), axis=1, keepdims=True)

    scale = lax.rsqrt(sums([proj * proj for proj in projs]) / size + epsilon)
    scores = sums([proj * val_dir for proj in projs]) * scale / math.sqrt(size)
    for e in range(examples):
        directions[e] = projs[e] * scale[e : e + 1]
        scores_out[e] = scores[e, 0]
    for j in range(k1):
        dirs_out[:, pl.ds(j * k2, k2)] = directions[:, j, :]


def chunk(slots, blocks, moments, x, g, columns, top, bottom, rank, last=None):
    tokens, width = x.shape
    k2 = columns.shape[1]
    span = width // slots.shape[0]
    examples = top.shape[0] // rank
    scratch = [
        pltpu.VMEM((2, (examples + 2) * rank, span), jnp.bfloat16),
        pltpu.VMEM((2, (examples + 2) * rank, 2 * k2), jnp.float32),
    ]
    common = [SMEM] + [VMEM] * (len(moments) + 5)
    operands = [slots, *moments, x, g, columns, top, bottom]
    options = dict(
        compiler_params=pltpu.CompilerParams(vmem_limit_bytes=CHUNK_LIMIT),
        cost_estimate=pl.CostEstimate(flops=10**6, bytes_accessed=10**6, transcendentals=0),
    )
    if last is None:
        return pl.pallas_call(
            functools.partial(chunk_kernel, blocks, len(moments)),
            in_specs=common,
            out_specs=VMEM,
            out_shape=jax.ShapeDtypeStruct((2, (examples + 1) * rank, k2), jnp.float32),
            scratch_shapes=scratch,
            name="chunk",
            **options,
        )(*operands)
    rows_t, val_parts, partials = last
    k1 = rows_t.shape[0]
    return pl.pallas_call(
        functools.partial(last_kernel, blocks, len(moments), len(val_parts), len(partials)),
        in_specs=common + [VMEM] * (1 + len(val_parts) + len(partials)),
        out_specs=[VMEM, VMEM, SMEM],
        out_shape=[
            jax.ShapeDtypeStruct((examples, k1 * k2), jnp.float32),
            jax.ShapeDtypeStruct((k1, k2), jnp.float32),
            jax.ShapeDtypeStruct((examples,), jnp.float32),
        ],
        scratch_shapes=[
            pltpu.VMEM((2 * rank, (examples + 1) * k2), jnp.float32),
            pltpu.VMEM((examples, k1, k2), jnp.float32),
            *scratch,
        ],
        name="last_chunk",
        **options,
    )(*operands, rows_t, *val_parts, *partials)


def slot_at(other, hop):
    return lambda: lax.bitwise_xor(lax.axis_index("shard"), 2 * hop + other)


def ordered_block(quarter, other, hop, which, place):
    return slot_at(other, hop), lambda moments, k: (moments[which], (2 * place + k) * quarter, quarter)


def paired_block(quarter, other, which):
    return slot_at(other, 0), lambda moments, k: (moments[2 * which + k], 0, quarter)


def gathered_block(quarter, b):
    return lambda: b, lambda moments, k: (moments[k].at[b], 0, quarter)


def exchange(value, axis, bits):
    size = lax.axis_size(axis)
    return lax.ppermute(value, axis, [(i, i ^ bits) for i in range(size)])


def body(
    training_inputs,
    training_cotangents,
    validation_inputs,
    validation_cotangents,
    adapter_down,
    adapter_up,
    adam_first_moment,
    adam_second_moment,
    slot_block_index,
    example_lengths,
    projection_rows,
    projection_columns,
):
    groups = lax.axis_size("dp")
    shards = lax.axis_size("shard")
    rank = adapter_up.shape[0]
    quarter = 2 * rank // groups
    stepwise = groups == 4 and shards == 8
    rows_t = projection_rows.T
    own = [m.reshape(groups, quarter, -1) for m in (adam_first_moment, adam_second_moment)]
    train = (training_inputs, training_cotangents)
    if stepwise:
        piece = cut_piece(*own)
        sibling = [exchange(m, "shard", 1) for m in own]
        far = [exchange(piece, "shard", 2 * hop) for hop in (1, 2, 3)]
        validation_inputs, _ = lax.optimization_barrier((validation_inputs, piece))
    down_t = adapter_down.T
    val_part = validation(
        validation_inputs, validation_cotangents, down_t, adapter_up, projection_columns, rows_t
    )
    lengths, val_part = lax.optimization_barrier((example_lengths[0, 0], val_part))
    top, bottom = prepare(lengths, *train, down_t, adapter_up)
    if stepwise:
        val_part, *sibling, far[0], far[1] = lax.optimization_barrier((val_part, *sibling, far[0], far[1]))
        packed = pack(far[0], val_part)
        near = [packed] + [exchange(packed, "dp", bits) for bits in (1, 2, 3)]
        *arrived, top, bottom = lax.optimization_barrier((*far[1:], *near, top, bottom))
        rest = join(*arrived[:2])
        four = [rest] + [exchange(rest, "dp", bits) for bits in (1, 2, 3)]
        one = order(arrived[2:])
        one, top, bottom = lax.optimization_barrier((one, top, bottom))
        one_crossed = exchange(one, "shard", 1)
        operands = (*train, projection_columns, top, bottom, rank)
        slots = slot_block_index
        partials = [chunk(slots, [paired_block(quarter, i, i) for i in (0, 1)], own + sibling, *operands)]
        partials[0], one_crossed = lax.optimization_barrier((partials[0], one_crossed))
        total = plane_sum(2 * quarter, val_part.shape, one, one_crossed)
        total, one_crossed = lax.optimization_barrier((total, one_crossed))
        other = exchange(total, "shard", 2)
        partials.append(
            chunk(slots, [ordered_block(quarter, i, 1, i, 0) for i in (0, 1)], [one, one_crossed], *operands)
        )
        partials[1], other, *four = lax.optimization_barrier((partials[1], other, *four))
        total = total + other
        both = order(four)
        total, both = lax.optimization_barrier((total, both))
        val_parts = [total, exchange(total, "shard", 4)]
        both_crossed = exchange(both, "shard", 1)
        partials.append(chunk(slots, [ordered_block(quarter, 0, 2 + i, 0, i) for i in (0, 1)], [both], *operands))
        dirs, val_dir, scores = chunk(
            slots,
            [ordered_block(quarter, 1, 2 + i, 0, i) for i in (0, 1)],
            [both_crossed],
            *operands,
            last=(rows_t, val_parts, partials),
        )
    else:
        operands = (*train, projection_columns, top, bottom, rank)
        gathered = [lax.all_gather(m, "shard", axis=0, tiled=False) for m in own]
        val_sum = lax.psum(val_part, ("dp", "shard"))
        dirs, val_dir, scores = chunk(
            slot_block_index,
            [gathered_block(quarter, b) for b in range(shards)],
            gathered,
            *operands,
            last=(rows_t, [val_sum], []),
        )
    return (
        dirs.reshape(1, 1, dirs.shape[0], -1),
        val_dir.reshape(-1),
        scores[None, None],
    )


def solution(mesh):
    return jax.shard_map(
        body,
        mesh=mesh,
        in_specs=(
            P(("dp", "shard"), None),
            P(("dp", "shard"), None),
            P(("dp", "shard"), None),
            P(("dp", "shard"), None),
            P(),
            P(),
            P("shard", None, None),
            P("shard", None, None),
            P(),
            P("dp", "shard", None),
            P(),
            P(),
        ),
        out_specs=(P("dp", "shard", None, None), P(), P("dp", "shard", None)),
        check_vma=False,
    )
```
